256 devices in a mesh: wave: 64 (over x, z, core), lev: 4 (over y).
Axes of the slice: x: 4, y: 4, z: 8, core: 2. Of those that a mesh axis runs over, the one named last changes fastest.
Arguments:
- fourier: bfloat16 [2, 2, 72, 1280, 640], P(None, None, 'lev', 'wave'), may hold values from -6 to 6
- lat_order: int32 [1280], replicated, may hold values from 0 to 1279, each once
- wave_order: int32 [640], replicated, may hold values from 0 to 639, as said below
- pattern: int32 [64, 64], replicated, may hold values from 0 to 1, as said below
- legendre: bfloat16 [640, 640, 640], P('wave'), may hold values from -0.25 to 0.25
- lat_weight: float32 [640], replicated, may hold values from 0.2 to 1.8
- hydrostatic_thermal_link: float32 [72, 72], replicated, may hold values from -0.75 to 0.75
- evec: float32 [72, 72], replicated, may hold values from -0.75 to 0.75
- einv: float32 [72, 72], replicated, may hold values from -0.75 to 0.75
- spread_to_heat_link: float32 [72, 72], replicated, may hold values from -0.75 to 0.75
- modes: float32 [72], replicated, may hold values from 0.5 to 50
Outputs:
- new_fourier: bfloat16 [2, 2, 72, 1280, 640], P(None, None, 'lev', 'wave')
The draws below stay inside these ranges and needn't reach their ends.
Inputs may be any that keep to these rules, and one draw needn't show every extreme that they name: `wave_order`: each wavenumber appears once; positions 2i and 2i+1 hold a wavenumber p and 639-p. pattern[i, j] is 1 where j >= i and 0 where j < i - 1.
All inputs are finite; a program needn't handle non-finite values.
Results may differ from the reference program's by a relative error of at most 0.0061.
Values may be sent and summed in bfloat16 or wider, within the bound.
No kernel may reach another device: no remote copies, remote signals or barrier semaphores. Data moves between devices by JAX's collectives and lax.ppermute only.
A program may use at most 128 MiB of HBM per device.

```python
import math
import jax
import jax.numpy as jnp
from jax import lax

M = 640
NBLK = 64
LEV = 72
FLD = 2
NLAT = 1280
NLAT_H = 640


def draw_wave_order(key, part):
    key = jax.random.fold_in(key, 11)
    paired = jax.random.permutation(key, M // 2).astype(jnp.int32)
    return jnp.stack([paired, M - 1 - paired], axis=1).reshape(M).astype(jnp.int32)


def draw_pattern(key, part):
    key = jax.random.fold_in(key, 23)
    reach = jax.random.randint(key, (NBLK,), 0, 2).astype(jnp.int32)
    row_ids = jnp.arange(NBLK, dtype=jnp.int32)[:, None]
    col_ids = jnp.arange(NBLK, dtype=jnp.int32)[None, :]
    return (col_ids >= row_ids - reach[:, None]).astype(jnp.int32)


def level_of(key, dims, cuts, least, top_value):
    def one(axis_at, parts):
        heights = jax.random.uniform(jax.random.fold_in(jax.random.fold_in(key, 6), axis_at), (parts,), jnp.float32, least / len(cuts), top_value / len(cuts))
        return jnp.repeat(jnp.exp(heights), dims[axis_at] // parts).reshape((-1,) + (1,) * (len(dims) - axis_at - 1))

    factor_of = one(*cuts[0])
    for cut in cuts[1:]:
        factor_of = factor_of * one(*cut)
    return factor_of


def bell_draw(rng, extent, width, most, cuts=(), held_as=jnp.bfloat16):
    values = width * jax.random.normal(rng, extent, jnp.float32)
    if cuts:
        values = values * level_of(rng, extent, cuts, -0.22, 0.18)
    return jnp.clip(values, -most, most).astype(held_as)


def setup_inputs(seed: int = 0) -> dict:
    key_list = jax.random.split(jax.random.key(seed), 12)
    return {
        "fourier": bell_draw(key_list[0], (FLD, 2, LEV, NLAT, M), 1.0, 6.0, ((2, 4), (3, 64))),
        "lat_order": jax.random.permutation(key_list[1], NLAT).astype(jnp.int32),
        "wave_order": draw_wave_order(jax.random.fold_in(key_list[11], 71), 0),
        "pattern": draw_pattern(jax.random.fold_in(key_list[11], 71), 0),
        "legendre": bell_draw(key_list[4], (M, M, NLAT_H), NLAT_H ** -0.5, 0.25, ((0, 64),)),
        "lat_weight": jnp.clip(jax.random.uniform(key_list[5], (NLAT_H,), jnp.float32, 0.2, 1.8), 0.2, 1.8),
        "hydrostatic_thermal_link": bell_draw(key_list[6], (LEV, LEV), LEV ** -0.5, 0.75, (), jnp.float32),
        "evec": bell_draw(key_list[7], (LEV, LEV), LEV ** -0.5, 0.75, (), jnp.float32),
        "einv": bell_draw(key_list[8], (LEV, LEV), LEV ** -0.5, 0.75, (), jnp.float32),
        "spread_to_heat_link": bell_draw(key_list[9], (LEV, LEV), LEV ** -0.5, 0.75, (), jnp.float32),
        "modes": jnp.clip(jnp.exp(jax.random.uniform(key_list[10], (LEV,), jnp.float32, math.log(0.5), math.log(50.0))), 0.5, 50.0),
    }


def solve_block(harmonic_amplitudes, degree_rows, hydrostatic_thermal_link, evec, einv, spread_to_heat_link, modes):
    maximal_order_cutoff = lax.Precision.HIGHEST
    velocity_spread = harmonic_amplitudes[:, :, 0].astype(jnp.float32)
    thermal_state = harmonic_amplitudes[:, :, 1].astype(jnp.float32)
    multiplier_entry = (degree_rows * (degree_rows + 1)).astype(jnp.float32) / float(M * (M + 1))
    multiplier_entry = multiplier_entry[None, :, None, None]
    source_drive = velocity_spread + multiplier_entry * jnp.einsum("apbg,og->apbo", thermal_state, hydrostatic_thermal_link, precision=maximal_order_cutoff)
    modal_part = jnp.einsum("apbg,og->apbo", source_drive, einv, precision=maximal_order_cutoff) / (1.0 + multiplier_entry * modes)
    next_velocity_spread = jnp.einsum("apbg,og->apbo", modal_part, evec, precision=maximal_order_cutoff)
    next_thermal_state = thermal_state - jnp.einsum("apbg,og->apbo", next_velocity_spread, spread_to_heat_link, precision=maximal_order_cutoff)
    return jnp.stack([next_velocity_spread, next_thermal_state], axis=2).astype(jnp.bfloat16)


def reference(fourier, lat_order, wave_order, pattern, legendre, lat_weight, hydrostatic_thermal_link, evec, einv, spread_to_heat_link, modes):
    maximal_order_cutoff = lax.Precision.HIGHEST
    lat_rows = jnp.arange(NLAT, dtype=jnp.int32)
    inverse_lat = jnp.zeros((NLAT,), jnp.int32).at[lat_order].set(lat_rows)
    north_vals = jnp.take(fourier, inverse_lat[:NLAT_H], axis=3).astype(jnp.float32)
    south_vals = jnp.take(fourier, inverse_lat[::-1][:NLAT_H], axis=3).astype(jnp.float32)
    weight = lat_weight[:, None]
    sym_part = ((north_vals + south_vals) * weight).astype(jnp.bfloat16)
    anti_part = ((north_vals - south_vals) * weight).astype(jnp.bfloat16)
    block_width = M // NBLK
    degrees = jnp.arange(M, dtype=jnp.int32)
    live_mask = pattern[wave_order // block_width][:, degrees // block_width].astype(jnp.float32)
    parity_even = ((degrees[None, :] - wave_order[:, None]) % 2) == 0

    def forward(wave_slot):
        wavenumber = wave_order[wave_slot]
        legendre_rows = legendre[wave_slot].astype(jnp.float32)
        sym_column = lax.dynamic_index_in_dim(sym_part, wavenumber, axis=4, keepdims=False).astype(jnp.float32)
        anti_column = lax.dynamic_index_in_dim(anti_part, wavenumber, axis=4, keepdims=False).astype(jnp.float32)
        sym_terms = jnp.einsum("nh,fclh->nfcl", legendre_rows, sym_column, precision=maximal_order_cutoff)
        anti_terms = jnp.einsum("nh,fclh->nfcl", legendre_rows, anti_column, precision=maximal_order_cutoff)
        chosen = jnp.where(parity_even[wave_slot][:, None, None, None], sym_terms, anti_terms)
        return chosen * live_mask[wave_slot][:, None, None, None]

    harmonic_amplitudes = lax.map(forward, degrees).astype(jnp.bfloat16)
    solved = solve_block(harmonic_amplitudes, degrees, hydrostatic_thermal_link, evec, einv, spread_to_heat_link, modes)

    def inverse(wave_slot):
        legendre_rows = legendre[wave_slot].astype(jnp.float32)
        masked = solved[wave_slot].astype(jnp.float32) * live_mask[wave_slot][:, None, None, None]
        signs = jnp.where(parity_even[wave_slot], 1.0, -1.0).astype(jnp.float32)
        north_new = jnp.einsum("nh,nfcl->fclh", legendre_rows, masked, precision=maximal_order_cutoff)
        south_new = jnp.einsum("nh,nfcl->fclh", legendre_rows, masked * signs[:, None, None, None], precision=maximal_order_cutoff)
        return jnp.concatenate([north_new, south_new[..., ::-1]], axis=3).astype(jnp.bfloat16)

    grids = lax.map(inverse, degrees)
    inverse_wave = jnp.zeros((M,), jnp.int32).at[wave_order].set(degrees)
    natural = jnp.take(grids, inverse_wave, axis=0)
    banded = jnp.take(natural, lat_order, axis=4)
    return jnp.moveaxis(banded, 0, 4)
```

```python
import jax
import jax.numpy as jnp
from jax import lax
from jax.experimental import pallas as pl
from jax.experimental.pallas import tpu as pltpu
from jax.sharding import PartitionSpec as P

RQ, R5 = 4, 5
X = 72
XP = 80
FL = 36
FLP = 40
LANES = 384
NT = (((1,), (1,)), ((), ()))
TN = (((0,), (0,)), ((), ()))
NN = (((1,), (0,)), ((), ()))
F32 = jnp.float32
BF16 = jnp.bfloat16


def dot(a, b, dims):
    return lax.dot_general(a, b, dims, preferred_element_type=F32)


def params():
    return pltpu.CompilerParams(vmem_limit_bytes=48 * 1024 * 1024)


def put_rows(scr, start, size, stride, values):
    width = scr.shape[2]
    for t in range(scr.shape[0]):
        scr[t, pl.ds(start, size, stride=stride), :] = values[:, t * width : (t + 1) * width]


def get_rows(scr, start, size, stride):
    tiles = [scr[t, pl.ds(start, size, stride=stride), :] for t in range(scr.shape[0])]
    return jnp.concatenate(tiles, axis=1)


def put_block(scr, block):
    width = scr.shape[2]
    for t in range(scr.shape[0]):
        part = block[:, :, t * width : (t + 1) * width].astype(F32)
        scr[t] = part.reshape(scr.shape[1:])


def get_block(scr, out_ref):
    width = scr.shape[2]
    for t in range(scr.shape[0]):
        part = scr[t].reshape(out_ref.shape[:2] + (width,))
        out_ref[:, :, t * width : (t + 1) * width] = part.astype(BF16)


def tiles_of(size):
    return (size // 128, 128) if size % 128 == 0 else (1, size)


def h_block(lat_half):
    return 128 if lat_half % 128 == 0 else lat_half


def wave_matrix(wave_ref):
    waves = wave_ref[...]
    count = waves.shape[0]
    ids = lax.broadcasted_iota(jnp.int32, (count, count), 1)
    return jnp.where(waves == ids, 1.0, 0.0).astype(BF16)


def fill_lat_matrix(lat_ref, ot_scr):
    lat_count = ot_scr.shape[0]
    half = lat_count // 2
    hb = h_block(half)
    lats = lat_ref[...]
    for block in range(half // hb):
        ids = lax.broadcasted_iota(jnp.int32, (hb, lat_count), 0) + block * hb
        north = jnp.where(lats == ids, 1.0, 0.0).astype(BF16)
        south = jnp.where(lats == lat_count - 1 - ids, 1.0, 0.0).astype(BF16)
        ot_scr[2 * block * hb : (2 * block + 1) * hb, :] = north
        ot_scr[(2 * block + 1) * hb : (2 * block + 2) * hb, :] = south


def select_kernel(wave_ref, x_ref, out_ref, scr):
    count = out_ref.shape[0]
    rows = out_ref.shape[1]
    m_local = rows // RQ
    onehot = wave_matrix(wave_ref)
    for rq in range(RQ):
        got = dot(onehot, x_ref[rq], NT)
        for kk in range(m_local):
            put_rows(scr, kk * RQ + rq, count, rows, got[kk * count : (kk + 1) * count])
    get_block(scr, out_ref)


def forward_kernel(r_ref, lat_ref, weight_ref, even_ref, odd_ref, leg_ref, out_ref, scr, ot_scr, rt_scr, sa_scr, sp_scr):
    step = pl.program_id(0)
    count, rows = r_ref.shape[0], r_ref.shape[1]
    m_local = rows // RQ
    half = ot_scr.shape[0] // 2
    hb = h_block(half)
    span = RQ * count

    @pl.when(step == 0)
    def _():
        put_block(scr, r_ref[...])
        fill_lat_matrix(lat_ref, ot_scr)
        for kk in range(m_local):
            part = jnp.concatenate(
                [get_rows(scr, kk * RQ + rq, count, rows) for rq in range(RQ)], axis=0
            )
            turned = part.T
            for r5 in range(R5):
                rt_scr[kk, :X, r5 * span : (r5 + 1) * span] = turned[r5 * X : (r5 + 1) * X].astype(BF16)
        lhs = rt_scr[...].reshape(m_local * XP, 2 * half)
        for block in range(half // hb):
            both = dot(lhs, ot_scr[2 * block * hb : (2 * block + 2) * hb, :], NT)
            north, south = both[:, :hb], both[:, hb:]
            weight = weight_ref[:, block * hb : (block + 1) * hb]
            sym = ((north + south) * weight).astype(BF16)
            anti = ((north - south) * weight).astype(BF16)
            sa_scr[:, :XP, block * hb : (block + 1) * hb] = sym.reshape(m_local, XP, hb)
            sa_scr[:, XP:, block * hb : (block + 1) * hb] = anti.reshape(m_local, XP, hb)

    for k2 in range(2):
        kk = 2 * step + k2
        terms = dot(sa_scr[kk], leg_ref[k2], NT)
        put_rows(sp_scr, 0, X, 1, terms[:X] * even_ref[kk] + terms[XP : XP + X] * odd_ref[kk])
        for c in range(2):
            picked = get_rows(sp_scr, c, FL, 2)
            picked = jnp.concatenate([picked, jnp.zeros((FLP - FL, picked.shape[1]), F32)], axis=0)
            out_ref[2 * k2 + c, 0] = picked.astype(BF16)


def split(values):
    high = values.astype(BF16)
    return high, (values - high.astype(F32)).astype(BF16)


def solve_kernel(r_ref, first_ref, second_ref, modes_ref, keep_ref, out_ref):
    waves = r_ref.shape[3]
    first_high, first_low = split(first_ref[...])
    second_high, second_low = split(second_ref[...])
    ids = lax.broadcasted_iota(jnp.int32, (1, waves), 1)
    factor = (ids * (ids + 1)).astype(F32) / float(waves * (waves + 1))
    scale = 1.0 / (1.0 + factor * modes_ref[...])
    for pair in range(r_ref.shape[1]):
        state = r_ref[:, pair].astype(F32).reshape(4 * FLP, waves)
        state_low = state.astype(BF16)
        both = dot(first_high, state_low, NN) + dot(first_low, state_low, NN)
        modal = (both[:X] + factor * both[X:]) * scale
        modal_high, modal_low = split(modal)
        new = (
            dot(second_high, modal_high, NN)
            + dot(second_high, modal_low, NN)
            + dot(second_low, modal_high, NN)
        )
        new = new + keep_ref[...] * state
        out_ref[:, pair] = new.reshape(4, FLP, waves).astype(BF16)


def inverse_kernel(v_ref, lat_ref, live_ref, signed_ref, leg_ref, out_ref, scr, ot_scr, ns_scr, v_scr, b_scr):
    step = pl.program_id(0)
    count, rows = out_ref.shape[0], out_ref.shape[1]
    m_local = rows // RQ
    half = ot_scr.shape[0] // 2
    hb = h_block(half)
    span = RQ * count

    @pl.when(step == 0)
    def _():
        fill_lat_matrix(lat_ref, ot_scr)
        v_scr[...] = jnp.zeros_like(v_scr)

    for k2 in range(2):
        kk = 2 * step + k2
        for c in range(2):
            put_rows(v_scr, c, FL, 2, v_ref[2 * k2 + c, 0].astype(F32)[:FL])
        values = get_rows(v_scr, 0, XP, 1)
        lhs = jnp.concatenate([values * live_ref[kk], values * signed_ref[kk]], axis=0).astype(BF16)
        grid = dot(lhs, leg_ref[k2], NN).astype(BF16)
        for block in range(half // hb):
            piece = grid[:, block * hb : (block + 1) * hb]
            ns_scr[kk, :, 2 * block * hb : (2 * block + 1) * hb] = piece[:XP]
            ns_scr[kk, :, (2 * block + 1) * hb : (2 * block + 2) * hb] = piece[XP:]

    @pl.when(step == pl.num_programs(0) - 1)
    def _():
        lhs = ns_scr[...].reshape(m_local * XP, 2 * half)
        for r5 in range(R5):
            band = dot(lhs, ot_scr[:, r5 * span : (r5 + 1) * span], NN)
            b_scr[:, r5 * X : (r5 + 1) * X, :] = band.reshape(m_local, XP, span)[:, :X]
        for kk in range(m_local):
            turned = b_scr[kk].T
            for rq in range(RQ):
                put_rows(scr, kk * RQ + rq, count, rows, turned[rq * count : (rq + 1) * count])
        get_block(scr, out_ref)


def restore_kernel(wave_ref, r_ref, out_ref, scr):
    count, rows = r_ref.shape[0], r_ref.shape[1]
    m_local = rows // RQ
    onehot = wave_matrix(wave_ref)
    put_block(scr, r_ref[...])
    for rq in range(RQ):
        part = jnp.concatenate(
            [get_rows(scr, kk * RQ + rq, count, rows) for kk in range(m_local)], axis=0
        )
        out_ref[rq] = dot(part.astype(BF16), onehot, TN)[: R5 * X].astype(BF16)


def whole(shape):
    return pl.BlockSpec(shape, lambda i: (0,) * len(shape))


def local(
    fourier,
    lat_order,
    wave_order,
    pattern,
    legendre,
    lat_weight,
    hydrostatic_thermal_link,
    evec,
    einv,
    spread_to_heat_link,
    modes,
):
    m_local, waves, lat_half = legendre.shape
    lat_count = 2 * lat_half
    count = waves // m_local
    rows = m_local * RQ
    pairs = m_local // 2
    block_count = pattern.shape[0]
    block_width = waves // block_count
    lev_local = fourier.shape[2]
    high = lax.Precision.HIGHEST

    wave_col = wave_order.reshape(count, m_local).T.reshape(waves, 1)
    lat_row = lat_order.reshape(count, RQ, R5).transpose(2, 1, 0).reshape(1, lat_count)
    weight_row = lat_weight.reshape(1, lat_half)

    my_waves = lax.dynamic_slice_in_dim(wave_order, lax.axis_index("wave") * m_local, m_local)
    degrees = jnp.arange(waves, dtype=jnp.int32)
    parity_even = (degrees[None, :] - my_waves[:, None]) % 2 == 0
    owner_rows = (
        my_waves[:, None] // block_width == jnp.arange(block_count, dtype=jnp.int32)[None, :]
    ).astype(F32)
    live_rows = jnp.dot(owner_rows, pattern.astype(F32), precision=high)
    live = jnp.repeat(live_rows, block_width, axis=1)
    even = jnp.where(parity_even, live, 0.0)[:, None, :]
    odd = jnp.where(parity_even, 0.0, live)[:, None, :]
    signed = jnp.where(parity_even, live, -live)[:, None, :]
    live = live[:, None, :]

    einv_link = jnp.dot(einv, hydrostatic_thermal_link, precision=high)
    heat_evec = jnp.dot(spread_to_heat_link, evec, precision=high)
    lev_count = LEVS = einv.shape[0] // lev_local
    first = jnp.stack([einv, einv_link]).reshape(2, X, lev_count, lev_local)
    eye2 = jnp.eye(2, dtype=F32)
    first = (first.transpose(0, 1, 2, 3)[:, :, :, None, :] * eye2[:, None, None, :, None])
    first = first.reshape(2 * X, lev_count, 2 * lev_local)
    first = jnp.pad(first, ((0, 0), (0, 0), (0, FLP - FL))).reshape(2 * X, lev_count * FLP)
    second = jnp.stack([evec, -heat_evec]).reshape(2, lev_count, lev_local, X)
    second = second.transpose(1, 0, 2, 3).reshape(lev_count, 2 * lev_local, X)
    second = jnp.pad(second, ((0, 0), (0, FLP - FL), (0, 0))).reshape(lev_count * FLP, X)
    place = jnp.arange(lev_count * FLP, dtype=jnp.int32) % FLP
    keep = ((place >= lev_local) & (place < 2 * lev_local)).astype(F32)[:, None]

    sent = fourier.reshape(2, 2, lev_local, RQ, R5, waves).transpose(3, 4, 0, 2, 1, 5)
    sent = jnp.pad(sent.reshape(RQ, R5 * X, waves), ((0, 0), (0, LANES - R5 * X), (0, 0)))
    block_scratch = pltpu.VMEM((LANES // 128, count * rows, 128), F32)
    block_shape = jax.ShapeDtypeStruct((count, rows, LANES), BF16)
    picked = pl.pallas_call(
        select_kernel,
        out_shape=block_shape,
        scratch_shapes=[block_scratch],
        compiler_params=params(),
        name="select_waves",
    )(wave_col, sent)
    arrived = lax.all_to_all(picked, "wave", split_axis=0, concat_axis=0, tiled=True)

    leg_spec = pl.BlockSpec((2, waves, lat_half), lambda i: (i, 0, 0))
    spec_shape = jax.ShapeDtypeStruct((4, pairs, FLP, waves), BF16)
    spec_spec = pl.BlockSpec((4, 1, FLP, waves), lambda i: (0, i, 0, 0))
    row_spec = whole((m_local, 1, waves))
    spectra = pl.pallas_call(
        forward_kernel,
        grid=(pairs,),
        in_specs=[
            whole((count, rows, LANES)),
            whole((1, lat_count)),
            whole((1, lat_half)),
            row_spec,
            row_spec,
            leg_spec,
        ],
        out_specs=spec_spec,
        out_shape=spec_shape,
        scratch_shapes=[
            block_scratch,
            pltpu.VMEM((lat_count, lat_count), BF16),
            pltpu.VMEM((m_local, XP, lat_count), BF16),
            pltpu.VMEM((m_local, 2 * XP, lat_half), BF16),
            pltpu.VMEM((tiles_of(waves)[0], X, tiles_of(waves)[1]), F32),
        ],
        compiler_params=params(),
        name="forward_legendre",
    )(arrived, lat_row, weight_row, even, odd, legendre)
    shifted = lax.all_to_all(spectra, "lev", split_axis=0, concat_axis=0, tiled=True)
    solved = pl.pallas_call(
        solve_kernel,
        out_shape=spec_shape,
        compiler_params=params(),
        name="solve_levels",
    )(shifted, first, second, modes[:, None], keep)
    back = lax.all_to_all(solved, "lev", split_axis=0, concat_axis=0, tiled=True)
    banded = pl.pallas_call(
        inverse_kernel,
        grid=(pairs,),
        in_specs=[
            spec_spec,
            whole((1, lat_count)),
            row_spec,
            row_spec,
            leg_spec,
        ],
        out_specs=whole((count, rows, LANES)),
        out_shape=block_shape,
        scratch_shapes=[
            block_scratch,
            pltpu.VMEM((lat_count, lat_count), BF16),
            pltpu.VMEM((m_local, XP, lat_count), BF16),
            pltpu.VMEM((tiles_of(waves)[0], XP, tiles_of(waves)[1]), F32),
            pltpu.VMEM((m_local, LANES, RQ * count), F32),
        ],
        compiler_params=params(),
        name="inverse_legendre",
    )(back, lat_row, live, signed, legendre)
    returned = lax.all_to_all(banded, "wave", split_axis=0, concat_axis=0, tiled=True)
    restored = pl.pallas_call(
        restore_kernel,
        out_shape=jax.ShapeDtypeStruct((RQ, R5 * X, waves), BF16),
        scratch_shapes=[block_scratch],
        compiler_params=params(),
        name="restore_waves",
    )(wave_col, returned)
    restored = restored.reshape(RQ, R5, 2, lev_local, 2, waves).transpose(2, 4, 3, 0, 1, 5)
    return restored.reshape(fourier.shape)


def solution(mesh):
    placed = (
        P(None, None, "lev", "wave", None),
        P(),
        P(),
        P(),
        P("wave", None, None),
        P(),
        P(),
        P(),
        P(),
        P(),
        P(),
    )
    return jax.shard_map(
        local,
        mesh=mesh,
        in_specs=placed,
        out_specs=P(None, None, "lev", "wave", None),
        check_vma=False,
    )
```

```python
import jax
import jax.numpy as jnp
from jax import lax
from jax.experimental import pallas as pl
from jax.experimental.pallas import tpu as pltpu
from jax.sharding import PartitionSpec as P

RQ, R5 = 4, 5
CUTS = 2
X = 72
XP = 80
FL = 36
FLP = 40
LANES = 384
NT = (((1,), (1,)), ((), ()))
TN = (((0,), (0,)), ((), ()))
NN = (((1,), (0,)), ((), ()))
F32 = jnp.float32
BF16 = jnp.bfloat16


def dot(a, b, dims):
    return lax.dot_general(a, b, dims, preferred_element_type=F32)


def params():
    return pltpu.CompilerParams(vmem_limit_bytes=26 * 1024 * 1024)


def put_rows(scr, start, size, stride, values):
    width = scr.shape[2]
    for t in range(scr.shape[0]):
        scr[t, pl.ds(start, size, stride=stride), :] = values[:, t * width : (t + 1) * width]


def get_rows(scr, start, size, stride):
    tiles = [scr[t, pl.ds(start, size, stride=stride), :] for t in range(scr.shape[0])]
    return jnp.concatenate(tiles, axis=1)


def put_block(scr, block):
    width = scr.shape[2]
    for t in range(scr.shape[0]):
        part = block[:, :, t * width : (t + 1) * width].astype(F32)
        scr[t] = part.reshape(scr.shape[1:])


def get_block(scr, out_ref):
    width = scr.shape[2]
    for t in range(scr.shape[0]):
        part = scr[t].reshape(out_ref.shape[:2] + (width,))
        out_ref[:, :, t * width : (t + 1) * width] = part.astype(BF16)


def tiles_of(size):
    return (size // 128, 128) if size % 128 == 0 else (1, size)


def h_block(lat_half):
    return 128 if lat_half % 128 == 0 else lat_half


def wave_matrix(wave_ref, m_local):
    count = wave_ref.shape[1]
    peers = count // m_local
    row = lax.broadcasted_iota(jnp.int32, (count, count), 0)
    ids = lax.broadcasted_iota(jnp.int32, (count, count), 1)
    slot = lax.rem(row, peers) * m_local + lax.div(row, peers)
    waves = wave_ref[...].astype(F32)
    held = jnp.sum(jnp.where(ids == slot, waves, 0.0), axis=1, keepdims=True)
    return jnp.where(held == ids.astype(F32), 1.0, 0.0).astype(BF16)


def fill_lat_matrix(lat_ref, ot_scr):
    lat_count = ot_scr.shape[0]
    half = lat_count // 2
    hb = h_block(half)
    lats = lat_ref[...]
    for block in range(half // hb):
        ids = lax.broadcasted_iota(jnp.int32, (hb, lat_count), 0) + block * hb
        north = jnp.where(lats == ids, 1.0, 0.0).astype(BF16)
        south = jnp.where(lats == lat_count - 1 - ids, 1.0, 0.0).astype(BF16)
        ot_scr[2 * block * hb : (2 * block + 1) * hb, :] = north
        ot_scr[(2 * block + 1) * hb : (2 * block + 2) * hb, :] = south


def lat_kernel(lat_ref, out_ref):
    fill_lat_matrix(lat_ref, out_ref)


def select_kernel(wave_ref, x_hbm, out_hbm, x_buf, z_scr, scr, out_buf, in_sem, out_sem):
    count, rows = out_buf.shape[0], out_buf.shape[1]
    m_local = rows // RQ
    loads = []
    for rq in range(RQ):
        part = pl.ds(rq * R5, R5)
        loads.append(pltpu.make_async_copy(x_hbm.at[:, part], x_buf.at[:, part], in_sem.at[rq]))
        loads[-1].start()
    onehot = wave_matrix(wave_ref, m_local)
    z_scr[R5 * X :, :] = jnp.zeros((LANES - R5 * X, z_scr.shape[1]), BF16)
    for rq in range(RQ):
        loads[rq].wait()
        for r5 in range(R5):
            piece = x_buf[:, rq * R5 + r5].reshape(X, z_scr.shape[1])
            z_scr[r5 * X : (r5 + 1) * X, :] = piece
        got = dot(onehot, z_scr[...], NT)
        for kk in range(m_local):
            put_rows(scr, kk * RQ + rq, count, rows, got[kk * count : (kk + 1) * count])
    step = count // CUTS
    width = scr.shape[2]
    stores = []
    for cut in range(CUTS):
        part = pl.ds(cut * step, step)
        for t in range(scr.shape[0]):
            lanes = pl.ds(t * width, width)
            piece = scr[t, pl.ds(cut * step * rows, step * rows), :].reshape(step, rows, width)
            out_buf[part, :, lanes] = piece.astype(BF16)
        stores.append(pltpu.make_async_copy(out_buf.at[part], out_hbm.at[part], out_sem.at[cut]))
        stores[-1].start()
    for store in stores:
        store.wait()


def forward_kernel(r_ref, ot_scr, weight_ref, even_ref, odd_ref, leg_ref, out_hbm, scr, rt_scr, sa_scr, sp_scr, out_ref, out_sem):
    count, rows = r_ref.shape[0], r_ref.shape[1]
    m_local = rows // RQ
    half = ot_scr.shape[0] // 2
    hb = h_block(half)
    span = RQ * count

    put_block(scr, r_ref[...])
    for kk in range(m_local):
        part = jnp.concatenate(
            [get_rows(scr, kk * RQ + rq, count, rows) for rq in range(RQ)], axis=0
        )
        turned = part.T
        for r5 in range(R5):
            rt_scr[kk, :X, r5 * span : (r5 + 1) * span] = turned[r5 * X : (r5 + 1) * X].astype(BF16)
    lhs = rt_scr[...].reshape(m_local * XP, 2 * half)
    for block in range(half // hb):
        both = dot(lhs, ot_scr[2 * block * hb : (2 * block + 2) * hb, :], NT)
        north, south = both[:, :hb], both[:, hb:]
        weight = weight_ref[:, block * hb : (block + 1) * hb]
        sym = ((north + south) * weight).astype(BF16)
        anti = ((north - south) * weight).astype(BF16)
        sa_scr[:, :XP, block * hb : (block + 1) * hb] = sym.reshape(m_local, XP, hb)
        sa_scr[:, XP:, block * hb : (block + 1) * hb] = anti.reshape(m_local, XP, hb)

    stores = []
    for kk in range(m_local):
        pair, k2 = kk // 2, kk % 2
        terms = dot(sa_scr[kk], leg_ref[kk], NT)
        put_rows(sp_scr, 0, X, 1, terms[:X] * even_ref[kk] + terms[XP : XP + X] * odd_ref[kk])
        for c in range(2):
            picked = get_rows(sp_scr, c, FL, 2)
            picked = jnp.concatenate([picked, jnp.zeros((FLP - FL, picked.shape[1]), F32)], axis=0)
            out_ref[pair, 2 * k2 + c] = picked.astype(BF16)
        if k2 == 1:
            stores.append(
                pltpu.make_async_copy(out_ref.at[pair], out_hbm.at[:, pair], out_sem.at[pair])
            )
            stores[-1].start()
    for store in stores:
        store.wait()


def split(values):
    high = values.astype(BF16)
    return high, (values - high.astype(F32)).astype(BF16)


def solve_kernel(r_ref, first_ref, second_ref, modes_ref, keep_ref, out_ref):
    waves = r_ref.shape[3]
    first_high, first_low = split(first_ref[...])
    second_high, second_low = split(second_ref[...])
    ids = lax.broadcasted_iota(jnp.int32, (1, waves), 1)
    factor = (ids * (ids + 1)).astype(F32) / float(waves * (waves + 1))
    scale = 1.0 / (1.0 + factor * modes_ref[...])
    for pair in range(r_ref.shape[1]):
        state = r_ref[:, pair].astype(F32).reshape(4 * FLP, waves)
        state_low = state.astype(BF16)
        both = dot(first_high, state_low, NN) + dot(first_low, state_low, NN)
        modal = (both[:X] + factor * both[X:]) * scale
        modal_high, modal_low = split(modal)
        new = (
            dot(second_high, modal_high, NN)
            + dot(second_high, modal_low, NN)
            + dot(second_low, modal_high, NN)
        )
        new = new + keep_ref[...] * state
        out_ref[:, pair] = new.reshape(4, FLP, waves).astype(BF16)


def inverse_kernel(v_ref, ot_scr, live_ref, signed_ref, leg_ref, out_ref, scr, ns_scr, v_scr, b_scr):
    count, rows = out_ref.shape[0], out_ref.shape[1]
    m_local = rows // RQ
    half = ot_scr.shape[0] // 2
    hb = h_block(half)
    span = RQ * count
    v_scr[...] = jnp.zeros_like(v_scr)
    for kk in range(m_local):
        pair, k2 = kk // 2, kk % 2
        for c in range(2):
            put_rows(v_scr, c, FL, 2, v_ref[2 * k2 + c, pair].astype(F32)[:FL])
        values = get_rows(v_scr, 0, XP, 1)
        lhs = jnp.concatenate([values * live_ref[kk], values * signed_ref[kk]], axis=0).astype(BF16)
        grid = dot(lhs, leg_ref[kk], NN).astype(BF16)
        for block in range(half // hb):
            piece = grid[:, block * hb : (block + 1) * hb]
            ns_scr[kk, :, 2 * block * hb : (2 * block + 1) * hb] = piece[:XP]
            ns_scr[kk, :, (2 * block + 1) * hb : (2 * block + 2) * hb] = piece[XP:]
    lhs = ns_scr[...].reshape(m_local * XP, 2 * half)
    for r5 in range(R5):
        band = dot(lhs, ot_scr[:, r5 * span : (r5 + 1) * span], NN)
        b_scr[:, r5 * X : (r5 + 1) * X, :] = band.reshape(m_local, XP, span)[:, :X]
    for kk in range(m_local):
        turned = b_scr[kk].T
        for rq in range(RQ):
            put_rows(scr, kk * RQ + rq, count, rows, turned[rq * count : (rq + 1) * count])
    get_block(scr, out_ref)


def restore_kernel(wave_ref, r_ref, out_hbm, scr, out_buf, out_sem):
    count, rows = r_ref.shape[0], r_ref.shape[1]
    m_local = rows // RQ
    waves = wave_ref.shape[1]
    onehot = wave_matrix(wave_ref, m_local)
    put_block(scr, r_ref[...])
    stores = []
    for rq in range(RQ):
        part = jnp.concatenate(
            [get_rows(scr, kk * RQ + rq, count, rows) for kk in range(m_local)], axis=0
        )
        got = dot(part.astype(BF16), onehot, TN).astype(BF16)
        for r5 in range(R5):
            piece = got[r5 * X : (r5 + 1) * X].reshape(FL, 2, waves)
            out_buf[:, rq * R5 + r5] = piece
        part = pl.ds(rq * R5, R5)
        stores.append(pltpu.make_async_copy(out_buf.at[:, part], out_hbm.at[:, part], out_sem.at[rq]))
        stores[-1].start()
    for store in stores:
        store.wait()


def local(
    fourier,
    lat_order,
    wave_order,
    pattern,
    legendre,
    lat_weight,
    hydrostatic_thermal_link,
    evec,
    einv,
    spread_to_heat_link,
    modes,
):
    m_local, waves, lat_half = legendre.shape
    lat_count = 2 * lat_half
    count = waves // m_local
    rows = m_local * RQ
    pairs = m_local // 2
    block_count = pattern.shape[0]
    block_width = waves // block_count
    lev_local = fourier.shape[2]
    high = lax.Precision.HIGHEST

    wave_row = wave_order.reshape(1, waves)
    lat_row = lat_order.reshape(count, RQ, R5).transpose(2, 1, 0).reshape(1, lat_count)
    weight_row = lat_weight.reshape(1, lat_half)

    my_waves = lax.dynamic_slice_in_dim(wave_order, lax.axis_index("wave") * m_local, m_local)
    degrees = jnp.arange(waves, dtype=jnp.int32)
    parity_even = (degrees[None, :] - my_waves[:, None]) % 2 == 0
    owner_rows = (
        my_waves[:, None] // block_width == jnp.arange(block_count, dtype=jnp.int32)[None, :]
    ).astype(F32)
    live_rows = jnp.dot(owner_rows, pattern.astype(F32), precision=high)
    live = jnp.repeat(live_rows, block_width, axis=1)
    even = jnp.where(parity_even, live, 0.0)[:, None, :]
    odd = jnp.where(parity_even, 0.0, live)[:, None, :]
    signed = jnp.where(parity_even, live, -live)[:, None, :]
    live = live[:, None, :]

    einv_link = jnp.dot(einv, hydrostatic_thermal_link, precision=high)
    heat_evec = jnp.dot(spread_to_heat_link, evec, precision=high)
    lev_count = LEVS = einv.shape[0] // lev_local
    first = jnp.stack([einv, einv_link]).reshape(2, X, lev_count, lev_local)
    eye2 = jnp.eye(2, dtype=F32)
    first = (first.transpose(0, 1, 2, 3)[:, :, :, None, :] * eye2[:, None, None, :, None])
    first = first.reshape(2 * X, lev_count, 2 * lev_local)
    first = jnp.pad(first, ((0, 0), (0, 0), (0, FLP - FL))).reshape(2 * X, lev_count * FLP)
    second = jnp.stack([evec, -heat_evec]).reshape(2, lev_count, lev_local, X)
    second = second.transpose(1, 0, 2, 3).reshape(lev_count, 2 * lev_local, X)
    second = jnp.pad(second, ((0, 0), (0, FLP - FL), (0, 0))).reshape(lev_count * FLP, X)
    place = jnp.arange(lev_count * FLP, dtype=jnp.int32) % FLP
    keep = ((place >= lev_local) & (place < 2 * lev_local)).astype(F32)[:, None]

    vmem = pl.BlockSpec(memory_space=pltpu.VMEM)
    anywhere = pl.BlockSpec(memory_space=pltpu.HBM)
    block_scratch = pltpu.VMEM((LANES // 128, count * rows, 128), F32)
    block_shape = jax.ShapeDtypeStruct((count, rows, LANES), BF16)
    rowed = (2 * lev_local, RQ * R5, 2, waves)
    picked = pl.pallas_call(
        select_kernel,
        in_specs=[vmem, anywhere],
        out_specs=anywhere,
        out_shape=block_shape,
        scratch_shapes=[
            pltpu.VMEM(rowed, BF16),
            pltpu.VMEM((LANES, waves), BF16),
            block_scratch,
            pltpu.VMEM(block_shape.shape, BF16),
            pltpu.SemaphoreType.DMA((RQ,)),
            pltpu.SemaphoreType.DMA((CUTS,)),
        ],
        compiler_params=params(),
        name="select_waves",
    )(wave_row, fourier.transpose(0, 2, 3, 1, 4).reshape(rowed))
    arrived = lax.all_to_all(picked, "wave", split_axis=0, concat_axis=0, tiled=True)
    lat_matrix = pl.pallas_call(
        lat_kernel,
        in_specs=[vmem],
        out_specs=vmem,
        out_shape=jax.ShapeDtypeStruct((lat_count, lat_count), BF16),
        compiler_params=params(),
        name="lat_matrix",
    )(lat_row)

    spec_shape = jax.ShapeDtypeStruct((4, pairs, FLP, waves), BF16)
    lane_tiles, lane_width = tiles_of(waves)
    spectra = pl.pallas_call(
        forward_kernel,
        in_specs=[vmem] * 6,
        out_specs=anywhere,
        out_shape=spec_shape,
        scratch_shapes=[
            block_scratch,
            pltpu.VMEM((m_local, XP, lat_count), BF16),
            pltpu.VMEM((m_local, 2 * XP, lat_half), BF16),
            pltpu.VMEM((lane_tiles, X, lane_width), F32),
            pltpu.VMEM((pairs, 4, FLP, waves), BF16),
            pltpu.SemaphoreType.DMA((pairs,)),
        ],
        compiler_params=params(),
        name="forward_legendre",
    )(arrived, lat_matrix, weight_row, even, odd, legendre)
    shifted = lax.all_to_all(spectra, "lev", split_axis=0, concat_axis=0, tiled=True)
    solved = pl.pallas_call(
        solve_kernel,
        in_specs=[vmem] * 5,
        out_specs=vmem,
        out_shape=spec_shape,
        compiler_params=params(),
        name="solve_levels",
    )(shifted, first, second, modes[:, None], keep)
    back = lax.all_to_all(solved, "lev", split_axis=0, concat_axis=0, tiled=True)
    banded = pl.pallas_call(
        inverse_kernel,
        in_specs=[vmem] * 5,
        out_specs=vmem,
        out_shape=block_shape,
        scratch_shapes=[
            block_scratch,
            pltpu.VMEM((m_local, XP, lat_count), BF16),
            pltpu.VMEM((lane_tiles, XP, lane_width), F32),
            pltpu.VMEM((m_local, LANES, RQ * count), F32),
        ],
        compiler_params=params(),
        name="inverse_legendre",
    )(back, lat_matrix, live, signed, legendre)
    returned = lax.all_to_all(banded, "wave", split_axis=0, concat_axis=0, tiled=True)
    restored = pl.pallas_call(
        restore_kernel,
        in_specs=[vmem] * 2,
        out_specs=anywhere,
        out_shape=jax.ShapeDtypeStruct(rowed, BF16),
        scratch_shapes=[
            block_scratch,
            pltpu.VMEM(rowed, BF16),
            pltpu.SemaphoreType.DMA((RQ,)),
        ],
        compiler_params=params(),
        name="restore_waves",
    )(wave_row, returned)
    restored = restored.reshape(2, lev_local, RQ * R5, 2, waves)
    return restored.transpose(0, 3, 1, 2, 4)


def solution(mesh):
    placed = (
        P(None, None, "lev", "wave", None),
        P(),
        P(),
        P(),
        P("wave", None, None),
        P(),
        P(),
        P(),
        P(),
        P(),
        P(),
    )
    return jax.shard_map(
        local,
        mesh=mesh,
        in_specs=placed,
        out_specs=P(None, None, "lev", "wave", None),
        check_vma=False,
    )
```

```python
import functools

import jax
import jax.numpy as jnp
from jax import lax
from jax.experimental import pallas as pl
from jax.experimental.pallas import tpu as pltpu
from jax.sharding import PartitionSpec as P

RQ, R5 = 4, 5
CUTS = 2
X = 72
XP = 80
FL = 36
FLP = 40
LEV = 4
GAP = 128
LANES = 384
NT = (((1,), (1,)), ((), ()))
TN = (((0,), (0,)), ((), ()))
NN = (((1,), (0,)), ((), ()))
F32 = jnp.float32
BF16 = jnp.bfloat16


def dot(a, b, dims):
    return lax.dot_general(a, b, dims, preferred_element_type=F32)


def params(mebibytes=50):
    return pltpu.CompilerParams(vmem_limit_bytes=mebibytes * 1024 * 1024)


def put_rows(scr, start, size, stride, values):
    width = scr.shape[2]
    for t in range(scr.shape[0]):
        scr[t, pl.ds(start, size, stride=stride), :] = values[:, t * width : (t + 1) * width]


def get_rows(scr, start, size, stride):
    tiles = [scr[t, pl.ds(start, size, stride=stride), :] for t in range(scr.shape[0])]
    return jnp.concatenate(tiles, axis=1)


def put_block(scr, block):
    width = scr.shape[2]
    for t in range(scr.shape[0]):
        part = block[:, :, t * width : (t + 1) * width].astype(F32)
        scr[t] = part.reshape(scr.shape[1:])


def get_block(scr, out_ref):
    width = scr.shape[2]
    for t in range(scr.shape[0]):
        part = scr[t].reshape(out_ref.shape[:2] + (width,))
        out_ref[:, :, t * width : (t + 1) * width] = part.astype(BF16)


def tiles_of(size):
    return (size // 128, 128) if size % 128 == 0 else (1, size)


def h_block(lat_half):
    return 128 if lat_half % 128 == 0 else lat_half


def wave_matrix(wave_ref, m_local):
    count = wave_ref.shape[0]
    peers = count // m_local
    row = lax.broadcasted_iota(jnp.int32, (count, count), 0)
    ids = lax.broadcasted_iota(jnp.int32, (count, count), 1)
    slot = lax.rem(row, peers) * m_local + lax.div(row, peers)
    waves = wave_ref[...].reshape(1, count).astype(F32)
    held = jnp.sum(jnp.where(ids == slot, waves, 0.0), axis=1, keepdims=True)
    return jnp.where(held == ids.astype(F32), 1.0, 0.0).astype(BF16)


def fill_lat_matrix(lat_ref, ot_scr):
    lat_count = ot_scr.shape[0]
    half = lat_count // 2
    hb = h_block(half)
    lats = lat_ref[...]
    for block in range(half // hb):
        ids = lax.broadcasted_iota(jnp.int32, (hb, lat_count), 0) + block * hb
        north = jnp.where(lats == ids, 1.0, 0.0).astype(BF16)
        south = jnp.where(lats == lat_count - 1 - ids, 1.0, 0.0).astype(BF16)
        ot_scr[2 * block * hb : (2 * block + 1) * hb, :] = north
        ot_scr[(2 * block + 1) * hb : (2 * block + 2) * hb, :] = south


def lat_kernel(lat_ref, out_ref):
    fill_lat_matrix(lat_ref, out_ref)


def select_kernel(wave_ref, x_hbm, out_hbm, x_buf, z_scr, scr, out_buf, in_sem, out_sem):
    count, rows = out_buf.shape[0], out_buf.shape[1]
    m_local = rows // RQ
    loads = []
    for rq in range(RQ):
        part = pl.ds(rq * R5, R5)
        loads.append(pltpu.make_async_copy(x_hbm.at[:, part], x_buf.at[:, part], in_sem.at[rq]))
        loads[-1].start()
    onehot = wave_matrix(wave_ref, m_local)
    z_scr[R5 * X :, :] = jnp.zeros((LANES - R5 * X, z_scr.shape[1]), BF16)
    for rq in range(RQ):
        loads[rq].wait()
        for r5 in range(R5):
            piece = x_buf[:, rq * R5 + r5].reshape(X, z_scr.shape[1])
            z_scr[r5 * X : (r5 + 1) * X, :] = piece
        got = dot(onehot, z_scr[...], NT)
        for kk in range(m_local):
            put_rows(scr, kk * RQ + rq, count, rows, got[kk * count : (kk + 1) * count])
    step = count // CUTS
    width = scr.shape[2]
    stores = []
    for cut in range(CUTS):
        part = pl.ds(cut * step, step)
        for t in range(scr.shape[0]):
            lanes = pl.ds(t * width, width)
            piece = scr[t, pl.ds(cut * step * rows, step * rows), :].reshape(step, rows, width)
            out_buf[part, :, lanes] = piece.astype(BF16)
        stores.append(pltpu.make_async_copy(out_buf.at[part], out_hbm.at[part], out_sem.at[cut]))
        stores[-1].start()
    for store in stores:
        store.wait()


def fetch_legendre(leg_hbm, leg_buf, leg_sem):
    loads = []
    for kk in range(leg_buf.shape[0]):
        loads.append(pltpu.make_async_copy(leg_hbm.at[kk], leg_buf.at[kk], leg_sem.at[kk]))
        loads[-1].start()
    return loads


def forward_kernel(
    place_ref, r_ref, ot_scr, weight_ref, even_ref, odd_ref, leg_hbm,
    out0, out1, out2, out3, scr, rt_scr, sa_scr, sp_scr, out_scr, leg_buf, leg_sem,
):
    count, rows = r_ref.shape[0], r_ref.shape[1]
    m_local = rows // RQ
    half = ot_scr.shape[0] // 2
    hb = h_block(half)
    span = RQ * count
    slots = 2 * out_scr.shape[3]
    loads = fetch_legendre(leg_hbm, leg_buf, leg_sem)
    put_block(scr, r_ref[...])
    for kk in range(m_local):
        part = jnp.concatenate(
            [get_rows(scr, kk * RQ + rq, count, rows) for rq in range(RQ)], axis=0
        )
        turned = part.T
        for r5 in range(R5):
            rt_scr[kk, :X, r5 * span : (r5 + 1) * span] = turned[r5 * X : (r5 + 1) * X].astype(BF16)
    lhs = rt_scr[...].reshape(m_local * XP, 2 * half)
    for block in range(half // hb):
        both = dot(lhs, ot_scr[2 * block * hb : (2 * block + 2) * hb, :], NT)
        north, south = both[:, :hb], both[:, hb:]
        weight = weight_ref[:, block * hb : (block + 1) * hb]
        sym = ((north + south) * weight).astype(BF16)
        anti = ((north - south) * weight).astype(BF16)
        sa_scr[:, :XP, block * hb : (block + 1) * hb] = sym.reshape(m_local, XP, hb)
        sa_scr[:, XP:, block * hb : (block + 1) * hb] = anti.reshape(m_local, XP, hb)

    for pair in range(m_local // 2):
        packed = jnp.zeros((X, slots), F32)
        for kk in (2 * pair, 2 * pair + 1):
            loads[kk].wait()
            terms = dot(sa_scr[kk], leg_buf[kk], NT)
            picked = terms[:X] * even_ref[kk] + terms[XP : XP + X] * odd_ref[kk]
            picked = jnp.concatenate([picked, jnp.zeros((X, GAP), F32)], axis=1)
            packed = packed + pltpu.roll(picked, place_ref[kk], 1)
        put_rows(sp_scr, 0, X, 1, packed)
        for c in range(2):
            part = get_rows(sp_scr, c, FL, 2)
            part = jnp.concatenate([part, jnp.zeros((FLP - FL, slots), F32)], axis=0).astype(BF16)
            out_scr[2 * c, pair] = part[:, : slots // 2]
            out_scr[2 * c + 1, pair] = part[:, slots // 2 :]
    me = place_ref[2 * m_local]
    for shift, out in enumerate((out0, out1, out2, out3)):
        out[...] = out_scr[lax.rem(me + shift, LEV)]


def split(values):
    high = values.astype(BF16)
    return high, (values - high.astype(F32)).astype(BF16)


def solve_kernel(
    place_ref, r0, r1, r2, r3, first_ref, second_ref, modes_ref, keep_ref,
    out0, out1, out2, out3, *, waves, m_local,
):
    pairs, _, width = r0.shape
    first_high, first_low = split(first_ref[...])
    second_high, second_low = split(second_ref[...])
    side = lax.rem(place_ref[2 * m_local], 2)
    slot = lax.broadcasted_iota(jnp.int32, (1, width), 1) + side * width
    for pair in range(pairs):
        lower = slot + place_ref[m_local + pairs + pair]
        degree = jnp.where(slot >= place_ref[m_local + pair], slot - GAP, lower)
        factor = (degree * (degree + 1)).astype(F32) / float(waves * (waves + 1))
        state = jnp.concatenate([r[pair].astype(F32) for r in (r0, r1, r2, r3)], axis=0)
        state_low = state.astype(BF16)
        both = dot(first_high, state_low, NN) + dot(first_low, state_low, NN)
        modal = (both[:X] + factor * both[X:]) / (1.0 + factor * modes_ref[...])
        modal_high, modal_low = split(modal)
        new = (
            dot(second_high, modal_high, NN)
            + dot(second_high, modal_low, NN)
            + dot(second_low, modal_high, NN)
        )
        new = new + keep_ref[...] * state
        for shift, out in enumerate((out0, out1, out2, out3)):
            out[pair] = new[shift * FLP : (shift + 1) * FLP].astype(BF16)


def inverse_kernel(
    place_ref, v0, v1, v2, v3, ot_scr, live_ref, signed_ref, leg_hbm,
    out_ref, scr, ns_scr, in_scr, v_scr, b_scr, leg_buf, leg_sem,
):
    count, rows = out_ref.shape[0], out_ref.shape[1]
    m_local = rows // RQ
    half = ot_scr.shape[0] // 2
    hb = h_block(half)
    span = RQ * count
    waves = live_ref.shape[2]
    loads = fetch_legendre(leg_hbm, leg_buf, leg_sem)
    me = place_ref[2 * m_local]
    for shift, value in enumerate((v0, v1, v2, v3)):
        in_scr[lax.rem(me + shift, LEV)] = value[...]
    v_scr[...] = jnp.zeros_like(v_scr)
    for kk in range(m_local):
        pair, k2 = kk // 2, kk % 2
        if k2 == 0:
            for c in range(2):
                part = jnp.concatenate([in_scr[2 * c, pair], in_scr[2 * c + 1, pair]], axis=1)
                put_rows(v_scr, c, FL, 2, part.astype(F32)[:FL])
            packed = get_rows(v_scr, 0, XP, 1)
        values = pltpu.roll(packed, waves + GAP - place_ref[kk], 1)[:, :waves]
        lhs = jnp.concatenate([values * live_ref[kk], values * signed_ref[kk]], axis=0).astype(BF16)
        loads[kk].wait()
        grid = dot(lhs, leg_buf[kk], NN).astype(BF16)
        for block in range(half // hb):
            piece = grid[:, block * hb : (block + 1) * hb]
            ns_scr[kk, :, 2 * block * hb : (2 * block + 1) * hb] = piece[:XP]
            ns_scr[kk, :, (2 * block + 1) * hb : (2 * block + 2) * hb] = piece[XP:]
    lhs = ns_scr[...].reshape(m_local * XP, 2 * half)
    for r5 in range(R5):
        band = dot(lhs, ot_scr[:, r5 * span : (r5 + 1) * span], NN)
        b_scr[:, r5 * X : (r5 + 1) * X, :] = band.reshape(m_local, XP, span)[:, :X]
    for kk in range(m_local):
        turned = b_scr[kk].T
        for rq in range(RQ):
            put_rows(scr, kk * RQ + rq, count, rows, turned[rq * count : (rq + 1) * count])
    get_block(scr, out_ref)


def restore_kernel(wave_ref, r_ref, out_hbm, scr, out_buf, out_sem):
    count, rows = r_ref.shape[0], r_ref.shape[1]
    m_local = rows // RQ
    waves = wave_ref.shape[0]
    onehot = wave_matrix(wave_ref, m_local)
    put_block(scr, r_ref[...])
    stores = []
    for rq in range(RQ):
        part = jnp.concatenate(
            [get_rows(scr, kk * RQ + rq, count, rows) for kk in range(m_local)], axis=0
        )
        got = dot(part.astype(BF16), onehot, TN).astype(BF16)
        for r5 in range(R5):
            piece = got[r5 * X : (r5 + 1) * X].reshape(FL, 2, waves)
            out_buf[:, rq * R5 + r5] = piece
        part = pl.ds(rq * R5, R5)
        stores.append(pltpu.make_async_copy(out_buf.at[:, part], out_hbm.at[:, part], out_sem.at[rq]))
        stores[-1].start()
    for store in stores:
        store.wait()


def turn(blocks, sign):
    sent = list(blocks)
    for shift in (2, 1, 3):
        route = [(i, (i + sign * shift) % LEV) for i in range(LEV)]
        sent[shift] = lax.ppermute(blocks[shift], "lev", route)
    return sent


def local(
    fourier,
    lat_order,
    wave_order,
    pattern,
    legendre,
    lat_weight,
    hydrostatic_thermal_link,
    evec,
    einv,
    spread_to_heat_link,
    modes,
):
    m_local, waves, lat_half = legendre.shape
    lat_count = 2 * lat_half
    count = waves // m_local
    rows = m_local * RQ
    pairs = m_local // 2
    block_count = pattern.shape[0]
    block_width = waves // block_count
    lev_local = fourier.shape[2]
    lev_count = LEV
    high = lax.Precision.HIGHEST

    lat_row = lat_order.reshape(count, RQ, R5).transpose(2, 1, 0).reshape(1, lat_count)
    weight_row = lat_weight.reshape(1, lat_half)

    my_waves = lax.dynamic_slice_in_dim(wave_order, lax.axis_index("wave") * m_local, m_local)
    degrees = jnp.arange(waves, dtype=jnp.int32)
    parity_even = (degrees[None, :] - my_waves[:, None]) % 2 == 0
    owner_rows = (
        my_waves[:, None] // block_width == jnp.arange(block_count, dtype=jnp.int32)[None, :]
    ).astype(F32)
    live_rows = jnp.dot(owner_rows, pattern.astype(F32), precision=high)
    live = jnp.repeat(live_rows, block_width, axis=1)
    even = jnp.where(parity_even, live, 0.0)[:, None, :]
    odd = jnp.where(parity_even, 0.0, live)[:, None, :]
    signed = jnp.where(parity_even, live, -live)[:, None, :]
    live = live[:, None, :]
    lev_index = lax.axis_index("lev")
    edge = (my_waves // block_width - 1) * block_width
    low = my_waves < waves // 2
    slots = waves + GAP
    offset = jnp.where(low, GAP, slots - edge)
    edges, lows = edge.reshape(pairs, 2), low.reshape(pairs, 2)
    limit = jnp.sum(jnp.where(lows, edges, 0), axis=1) + GAP // 2 + block_width
    upper = jnp.sum(jnp.where(lows, 0, edges), axis=1)
    places = jnp.concatenate([offset, limit, upper, lev_index[None]]).astype(jnp.int32)

    def from_me(blocks, axis):
        back = jnp.flip(blocks, axis)
        twice = jnp.concatenate([back, back], axis)
        return lax.dynamic_slice_in_dim(twice, lev_count - 1 - lev_index, lev_count, axis)

    einv_link = jnp.dot(einv, hydrostatic_thermal_link, precision=high)
    heat_evec = jnp.dot(spread_to_heat_link, evec, precision=high)
    first = jnp.stack([einv, einv_link]).reshape(2, X, lev_count, lev_local)
    eye2 = jnp.eye(2, dtype=F32)
    first = (first.transpose(0, 1, 2, 3)[:, :, :, None, :] * eye2[:, None, None, :, None])
    first = first.reshape(2 * X, lev_count, 2 * lev_local)
    first = jnp.pad(first, ((0, 0), (0, 0), (0, FLP - FL)))
    first = from_me(first, 1).reshape(2 * X, lev_count * FLP)
    second = jnp.stack([evec, -heat_evec]).reshape(2, lev_count, lev_local, X)
    second = second.transpose(1, 0, 2, 3).reshape(lev_count, 2 * lev_local, X)
    second = jnp.pad(second, ((0, 0), (0, FLP - FL), (0, 0)))
    second = from_me(second, 0).reshape(lev_count * FLP, X)
    place = jnp.arange(lev_count * FLP, dtype=jnp.int32) % FLP
    keep = ((place >= lev_local) & (place < 2 * lev_local)).astype(F32)[:, None]

    vmem = pl.BlockSpec(memory_space=pltpu.VMEM)
    anywhere = pl.BlockSpec(memory_space=pltpu.HBM)
    block_scratch = pltpu.VMEM((LANES // 128, count * rows, 128), F32)
    block_shape = jax.ShapeDtypeStruct((count, rows, LANES), BF16)
    rowed = (2 * lev_local, RQ * R5, 2, waves)
    picked = pl.pallas_call(
        select_kernel,
        in_specs=[vmem, anywhere],
        out_specs=anywhere,
        out_shape=block_shape,
        scratch_shapes=[
            pltpu.VMEM(rowed, BF16),
            pltpu.VMEM((LANES, waves), BF16),
            block_scratch,
            pltpu.VMEM(block_shape.shape, BF16),
            pltpu.SemaphoreType.DMA((RQ,)),
            pltpu.SemaphoreType.DMA((CUTS,)),
        ],
        compiler_params=params(60),
        name="select_waves",
    )(wave_order, fourier.transpose(0, 2, 3, 1, 4).reshape(rowed))
    arrived = lax.all_to_all(picked, "wave", split_axis=0, concat_axis=0, tiled=True)
    lat_matrix = pl.pallas_call(
        lat_kernel,
        in_specs=[vmem],
        out_specs=vmem,
        out_shape=jax.ShapeDtypeStruct((lat_count, lat_count), BF16),
        compiler_params=params(),
        name="lat_matrix",
    )(lat_row)

    modes_col = modes[:, None]
    lat_matrix, weight_row, even, odd, live, signed, first, second, modes_col, keep, places = (
        lax.optimization_barrier(
            (lat_matrix, weight_row, even, odd, live, signed, first, second, modes_col, keep, places)
        )
    )

    smem = pl.BlockSpec(memory_space=pltpu.SMEM)
    spec_shape = jax.ShapeDtypeStruct((pairs, FLP, slots // 2), BF16)
    lane_tiles, lane_width = tiles_of(slots)
    leg_scratch = [
        pltpu.VMEM(legendre.shape, BF16),
        pltpu.SemaphoreType.DMA((m_local,)),
    ]
    spectra = pl.pallas_call(
        forward_kernel,
        in_specs=[smem] + [vmem] * 5 + [anywhere],
        out_specs=[vmem] * LEV,
        out_shape=[spec_shape] * LEV,
        scratch_shapes=[
            block_scratch,
            pltpu.VMEM((m_local, XP, lat_count), BF16),
            pltpu.VMEM((m_local, 2 * XP, lat_half), BF16),
            pltpu.VMEM((lane_tiles, X, lane_width), F32),
            pltpu.VMEM((LEV,) + spec_shape.shape, BF16),
        ]
        + leg_scratch,
        compiler_params=params(),
        name="forward_legendre",
    )(places, arrived, lat_matrix, weight_row, even, odd, legendre)
    shifted = turn(spectra, 1)
    solved = pl.pallas_call(
        functools.partial(solve_kernel, waves=waves, m_local=m_local),
        in_specs=[smem] + [vmem] * (LEV + 4),
        out_specs=[vmem] * LEV,
        out_shape=[spec_shape] * LEV,
        compiler_params=params(),
        name="solve_levels",
    )(places, *shifted, first, second, modes_col, keep)
    back = turn(solved, -1)
    banded = pl.pallas_call(
        inverse_kernel,
        in_specs=[smem] + [vmem] * (LEV + 3) + [anywhere],
        out_specs=vmem,
        out_shape=block_shape,
        scratch_shapes=[
            block_scratch,
            pltpu.VMEM((m_local, XP, lat_count), BF16),
            pltpu.VMEM((LEV,) + spec_shape.shape, BF16),
            pltpu.VMEM((lane_tiles, XP, lane_width), F32),
            pltpu.VMEM((m_local, LANES, RQ * count), F32),
        ]
        + leg_scratch,
        compiler_params=params(),
        name="inverse_legendre",
    )(places, *back, lat_matrix, live, signed, legendre)
    returned = lax.all_to_all(banded, "wave", split_axis=0, concat_axis=0, tiled=True)
    restored = pl.pallas_call(
        restore_kernel,
        in_specs=[vmem] * 2,
        out_specs=anywhere,
        out_shape=jax.ShapeDtypeStruct(rowed, BF16),
        scratch_shapes=[
            block_scratch,
            pltpu.VMEM(rowed, BF16),
            pltpu.SemaphoreType.DMA((RQ,)),
        ],
        compiler_params=params(),
        name="restore_waves",
    )(wave_order, returned)
    restored = restored.reshape(2, lev_local, RQ * R5, 2, waves)
    return restored.transpose(0, 3, 1, 2, 4)


def solution(mesh):
    placed = (
        P(None, None, "lev", "wave", None),
        P(),
        P(),
        P(),
        P("wave", None, None),
        P(),
        P(),
        P(),
        P(),
        P(),
        P(),
    )
    return jax.shard_map(
        local,
        mesh=mesh,
        in_specs=placed,
        out_specs=P(None, None, "lev", "wave", None),
        check_vma=False,
    )
```

```python
import jax
import jax.numpy as jnp
from jax import lax
from jax.experimental import pallas as pl
from jax.experimental.pallas import tpu as pltpu
from jax.sharding import PartitionSpec as P

RQ, R5 = 4, 5
ROWS = 8
LANES = 512
LEV = 4
LOCAL = 18
X = LEV * LOCAL
FL = 2 * LOCAL
UNIT = 40
XP = LEV * UNIT
SHARE = 5
GROUP = R5 * UNIT
WIDE = 2 * LANES
CUTS = 2
NT = (((1,), (1,)), ((), ()))
TN = (((0,), (0,)), ((), ()))
NN = (((1,), (0,)), ((), ()))
F32 = jnp.float32
BF16 = jnp.bfloat16


def dot(a, b, dims):
    return lax.dot_general(a, b, dims, preferred_element_type=F32)


def params(mebibytes):
    return pltpu.CompilerParams(vmem_limit_bytes=mebibytes * 1024 * 1024)


def put_rows(scr, start, size, stride, values):
    width = scr.shape[2]
    for t in range(scr.shape[0]):
        scr[t, pl.ds(start, size, stride=stride), :] = values[:, t * width : (t + 1) * width]


def get_rows(scr, start, size, stride):
    tiles = [scr[t, pl.ds(start, size, stride=stride), :] for t in range(scr.shape[0])]
    return jnp.concatenate(tiles, axis=1)


def put_block(scr, block):
    width = scr.shape[2]
    for t in range(scr.shape[0]):
        part = block[:, :, t * width : (t + 1) * width].astype(F32)
        scr[t] = part.reshape(scr.shape[1:])


def send_block(scr, out_buf, out_hbm, out_sem):
    width = scr.shape[2]
    peers, rows = out_buf.shape[0], out_buf.shape[1]
    step = peers // CUTS
    stores = []
    for cut in range(CUTS):
        part = pl.ds(cut * step, step)
        for t in range(scr.shape[0]):
            piece = scr[t, pl.ds(cut * step * rows, step * rows), :].reshape(step, rows, width)
            out_buf[part, :, pl.ds(t * width, width)] = piece.astype(BF16)
        stores.append(pltpu.make_async_copy(out_buf.at[part], out_hbm.at[part], out_sem.at[cut]))
        stores[-1].start()
    for store in stores:
        store.wait()


def tiles_of(size):
    return (size // 128, 128) if size % 128 == 0 else (1, size)


def h_block(lat_half):
    return 128 if lat_half % 128 == 0 else lat_half


def wave_matrix(wave_ref, peers):
    count = wave_ref.shape[0]
    m_local = count // peers
    row = lax.broadcasted_iota(jnp.int32, (count, 1), 0)
    ids = lax.broadcasted_iota(jnp.int32, (count, count), 1)
    slot = lax.rem(row, peers) * m_local + lax.div(row, peers)
    waves = wave_ref[...].reshape(1, count).astype(F32)
    held = jnp.sum(jnp.where(ids == slot, waves, 0.0), axis=1, keepdims=True)
    return jnp.where(held == ids.astype(F32), 1.0, 0.0).astype(BF16)


def fill_lat_matrix(rows_ref, ot_scr):
    lat_count = ot_scr.shape[0]
    half = lat_count // 2
    hb = h_block(half)
    at = rows_ref.shape[0] - 3
    lats = jnp.concatenate([rows_ref[at : at + 1, :], rows_ref[at + 1 : at + 2, :]], axis=1)
    lats = lats.astype(jnp.int32)
    for block in range(half // hb):
        ids = lax.broadcasted_iota(jnp.int32, (hb, lat_count), 0) + block * hb
        north = jnp.where(lats == ids, 1.0, 0.0).astype(BF16)
        south = jnp.where(lats == lat_count - 1 - ids, 1.0, 0.0).astype(BF16)
        ot_scr[2 * block * hb : (2 * block + 1) * hb, :] = north
        ot_scr[(2 * block + 1) * hb : (2 * block + 2) * hb, :] = south


def pieces_of(peer):
    pieces = []
    for combo in range(SHARE * peer, SHARE * (peer + 1)):
        kk, c = combo // 2, combo % 2
        if pieces and pieces[-1][0] == kk:
            pieces[-1] = (kk, 0, 2)
        else:
            pieces.append((kk, c, c + 1))
    return pieces


def select_kernel(wave_ref, x_hbm, out_hbm, x_buf, x_scr, z_scr, scr, out_buf, in_sem, out_sem):
    waves = z_scr.shape[1]
    peers = out_buf.shape[0] // LEV
    loads = []
    for rq in range(RQ):
        part = pl.ds(rq * R5, R5)
        loads.append(pltpu.make_async_copy(x_hbm.at[:, part], x_buf.at[:, part], in_sem.at[rq]))
        loads[-1].start()
    onehot = wave_matrix(wave_ref, peers)
    for rq in range(RQ):
        loads[rq].wait()
        for r5 in range(R5):
            piece = x_buf[:, rq * R5 + r5].astype(F32).reshape(2 * FL, waves)
            put_rows(x_scr, 0, 2 * FL, 1, piece)
            for c in range(2):
                part = get_rows(x_scr, c, FL, 2)
                part = jnp.concatenate([part, jnp.zeros((UNIT - FL, waves), F32)], axis=0)
                at = c * GROUP + r5 * UNIT
                z_scr[at : at + UNIT, :] = part.astype(BF16)
        got = dot(onehot, z_scr[...], NT)
        for peer in range(LEV):
            parts = [
                got[kk * peers : (kk + 1) * peers, low * GROUP : high * GROUP]
                for kk, low, high in pieces_of(peer)
            ]
            parts.append(jnp.zeros((peers, WIDE - SHARE * GROUP), F32))
            row = jnp.concatenate(parts, axis=1)
            for side in range(2):
                start = peer * ROWS + rq * 2 + side
                put_rows(scr, start, peers, LEV * ROWS, row[:, side * LANES : (side + 1) * LANES])
    send_block(scr, out_buf, out_hbm, out_sem)


def split(values):
    high = values.astype(BF16)
    return high, (values - high.astype(F32)).astype(BF16)


def spectral_kernel(
    place_ref, r_ref, rows_ref, vert_ref, leg_hbm, out_ref,
    ot_scr, scr, lat_scr, sa_scr, band_scr, leg_buf, leg_sem,
):
    peers = r_ref.shape[0] // LEV
    half = ot_scr.shape[0] // 2
    hb = h_block(half)
    span = 2 * peers
    waves = rows_ref.shape[1]
    me = place_ref[place_ref.shape[0] - 1]
    odd_me = lax.rem(me, 2)
    base = lax.div(me * SHARE, 2)
    loads = []
    for i in range(leg_buf.shape[0]):
        loads.append(pltpu.make_async_copy(leg_hbm.at[base + i], leg_buf.at[i], leg_sem.at[i]))
        loads[-1].start()
    fill_lat_matrix(rows_ref, ot_scr)
    put_block(scr, r_ref[...])
    for p in range(LEV):
        for pair in range(RQ // 2):
            part = jnp.concatenate(
                [
                    jnp.concatenate(
                        [get_rows(scr, p * ROWS + 2 * rq + side, peers, LEV * ROWS) for side in range(2)],
                        axis=1,
                    )
                    for rq in (2 * pair, 2 * pair + 1)
                ],
                axis=0,
            )
            turned = part.T
            for j in range(SHARE):
                for r5 in range(R5):
                    at = (j * R5 + r5) * UNIT
                    lane = (r5 * 2 + pair) * span
                    lat_scr[j, p * UNIT : (p + 1) * UNIT, lane : lane + span] = turned[at : at + UNIT].astype(BF16)
    lhs = lat_scr[...].reshape(SHARE * XP, 2 * half)
    for block in range(half // hb):
        both = dot(lhs, ot_scr[2 * block * hb : (2 * block + 2) * hb, :], NT)
        north, south = both[:, :hb], both[:, hb:]
        weight = rows_ref[rows_ref.shape[0] - 1 :, block * hb : (block + 1) * hb]
        sym = ((north + south) * weight).astype(BF16)
        anti = ((north - south) * weight).astype(BF16)
        sa_scr[:, :XP, block * hb : (block + 1) * hb] = sym.reshape(SHARE, XP, hb)
        sa_scr[:, XP:, block * hb : (block + 1) * hb] = anti.reshape(SHARE, XP, hb)

    first_high, first_low = split(vert_ref[: 2 * X, :])
    second_high, second_low = split(vert_ref[2 * X :, :X])
    keep = vert_ref[2 * X :, X : X + 1]
    modes = vert_ref[2 * X : 3 * X, X + 1 : X + 2]
    degree = lax.broadcasted_iota(jnp.int32, (1, waves), 1)
    factor = (degree * (degree + 1)).astype(F32) / float(waves * (waves + 1))
    scale = 1.0 + factor * modes
    for load in loads:
        load.wait()
    for j in range(SHARE):
        slot = lax.div(j + odd_me, 2)
        live = rows_ref[pl.ds(base + slot, 1), :]
        even = lax.rem(degree + place_ref[base + slot], 2) == 0
        leg = leg_buf[slot]
        terms = dot(sa_scr[j], leg, NT)
        state_low = (jnp.where(even, terms[:XP], terms[XP:]) * live).astype(BF16)
        state = state_low.astype(F32)
        mixed = dot(first_high, state_low, NN) + dot(first_low, state_low, NN)
        modal = (mixed[:X] + factor * mixed[X:]) / scale
        modal_high, modal_low = split(modal)
        new = (
            dot(second_high, modal_high, NN)
            + dot(second_high, modal_low, NN)
            + dot(second_low, modal_high, NN)
        )
        new = (new + keep * state).astype(BF16).astype(F32) * live
        signed = jnp.where(even, new, -new)
        grid = dot(jnp.concatenate([new, signed], axis=0).astype(BF16), leg, NN).astype(BF16)
        for block in range(half // hb):
            piece = grid[:, block * hb : (block + 1) * hb]
            lat_scr[j, :, 2 * block * hb : (2 * block + 1) * hb] = piece[:XP]
            lat_scr[j, :, (2 * block + 1) * hb : (2 * block + 2) * hb] = piece[XP:]

    lhs = lat_scr[...].reshape(SHARE * XP, 2 * half)
    for r5 in range(R5):
        band = dot(lhs, ot_scr[:, 2 * r5 * span : 2 * (r5 + 1) * span], NN)
        for j in range(SHARE):
            for p in range(LEV):
                at = (j * R5 + r5) * UNIT
                row = j * XP + p * UNIT
                band_scr[p, at : at + UNIT, :] = band[row : row + UNIT]
    for p in range(LEV):
        for pair in range(RQ // 2):
            turned = band_scr[p, :, pair * span : (pair + 1) * span].T
            for i in range(2):
                for side in range(2):
                    start = p * ROWS + (2 * pair + i) * 2 + side
                    piece = turned[i * peers : (i + 1) * peers, side * LANES : (side + 1) * LANES]
                    put_rows(scr, start, peers, LEV * ROWS, piece)
    width = scr.shape[2]
    for t in range(scr.shape[0]):
        part = scr[t].reshape(out_ref.shape[:2] + (width,))
        out_ref[:, :, t * width : (t + 1) * width] = part.astype(BF16)


def restore_kernel(wave_ref, r_ref, out_hbm, scr, y_scr, out_buf, out_sem):
    peers = r_ref.shape[0] // LEV
    waves = wave_ref.shape[0]
    onehot = wave_matrix(wave_ref, peers)
    put_block(scr, r_ref[...])
    stores = []
    for rq in range(RQ):
        held = {}
        for peer in range(LEV):
            row = jnp.concatenate(
                [get_rows(scr, peer * ROWS + rq * 2 + side, peers, LEV * ROWS) for side in range(2)],
                axis=1,
            )
            at = 0
            for kk, low, high in pieces_of(peer):
                size = (high - low) * GROUP
                held.setdefault(kk, []).append(row[:, at : at + size])
                at += size
        parts = [jnp.concatenate(held[kk], axis=1) for kk in sorted(held)]
        part = jnp.concatenate(parts, axis=0).astype(BF16)
        got = dot(part, onehot, TN)
        for r5 in range(R5):
            for c in range(2):
                at = c * GROUP + r5 * UNIT
                put_rows(y_scr, c, FL, 2, got[at : at + FL])
            piece = get_rows(y_scr, 0, 2 * FL, 1).astype(BF16)
            out_buf[:, rq * R5 + r5] = piece.reshape(FL, 2, waves)
        part = pl.ds(rq * R5, R5)
        stores.append(pltpu.make_async_copy(out_buf.at[:, part], out_hbm.at[:, part], out_sem.at[rq]))
        stores[-1].start()
    for store in stores:
        store.wait()


def local(
    fourier,
    lat_order,
    wave_order,
    pattern,
    legendre,
    lat_weight,
    hydrostatic_thermal_link,
    evec,
    einv,
    spread_to_heat_link,
    modes,
):
    m_local, waves, lat_half = legendre.shape
    lat_count = 2 * lat_half
    count = waves // m_local
    block_count = pattern.shape[0]
    block_width = waves // block_count
    high = lax.Precision.HIGHEST

    lat_rows = lat_order.reshape(count, RQ, R5).transpose(2, 1, 0).reshape(2, lat_half).astype(F32)
    my_waves = lax.dynamic_slice_in_dim(wave_order, lax.axis_index("wave") * m_local, m_local)
    owner_rows = (
        my_waves[:, None] // block_width == jnp.arange(block_count, dtype=jnp.int32)[None, :]
    ).astype(F32)
    live_rows = jnp.dot(owner_rows, pattern.astype(F32), precision=high)
    live = jnp.repeat(live_rows, block_width, axis=1)
    rows_in = jnp.concatenate([live, lat_rows, lat_weight[None, :]], axis=0)
    places = jnp.concatenate([my_waves, lax.axis_index("lev")[None]]).astype(jnp.int32)

    einv_link = jnp.dot(einv, hydrostatic_thermal_link, precision=high)
    heat_evec = jnp.dot(spread_to_heat_link, evec, precision=high)
    gap = ((0, 0), (0, UNIT - FL), (0, 0))
    none = jnp.zeros((X, LEV, LOCAL), F32)
    tail = jnp.zeros((X, LEV, UNIT - FL), F32)
    first = jnp.concatenate(
        [
            jnp.concatenate([einv.reshape(X, LEV, LOCAL), none, tail], axis=2),
            jnp.concatenate([none, einv_link.reshape(X, LEV, LOCAL), tail], axis=2),
        ],
        axis=0,
    ).reshape(2 * X, XP)
    second = jnp.concatenate(
        [evec.reshape(LEV, LOCAL, X), -heat_evec.reshape(LEV, LOCAL, X)], axis=1
    )
    second = jnp.pad(second, gap).reshape(XP, X)
    place = jnp.arange(XP, dtype=jnp.int32) % UNIT
    keep = ((place >= LOCAL) & (place < FL)).astype(F32)[:, None]
    column = jnp.arange(XP, dtype=jnp.int32)[None, :]
    second = jnp.pad(second, ((0, 0), (0, XP - X))) + keep * (column == X).astype(F32)
    second = second + jnp.pad(modes, (0, XP - X))[:, None] * (column == X + 1).astype(F32)
    vert = jnp.concatenate([first, second], axis=0)

    vmem = pl.BlockSpec(memory_space=pltpu.VMEM)
    smem = pl.BlockSpec(memory_space=pltpu.SMEM)
    hbm = pl.BlockSpec(memory_space=pltpu.HBM)
    peers = count * LEV
    rowed = (FL, RQ * R5, 2, waves)
    block = jax.ShapeDtypeStruct((peers, ROWS, LANES), BF16)
    block_scratch = pltpu.VMEM((LANES // 128, peers * ROWS, 128), F32)
    lane_tiles, lane_width = tiles_of(waves)
    row_scratch = pltpu.VMEM((lane_tiles, 2 * FL, lane_width), F32)

    sent = pl.pallas_call(
        select_kernel,
        in_specs=[vmem, hbm],
        out_specs=hbm,
        out_shape=block,
        scratch_shapes=[
            pltpu.VMEM(rowed, BF16),
            row_scratch,
            pltpu.VMEM((2 * GROUP, waves), BF16),
            block_scratch,
            pltpu.VMEM(block.shape, BF16),
            pltpu.SemaphoreType.DMA((RQ,)),
            pltpu.SemaphoreType.DMA((CUTS,)),
        ],
        compiler_params=params(60),
        name="select_waves",
    )(wave_order, fourier.transpose(0, 2, 3, 1, 4).reshape(rowed))
    arrived = lax.all_to_all(sent, ("wave", "lev"), split_axis=0, concat_axis=0, tiled=True)
    solved = pl.pallas_call(
        spectral_kernel,
        in_specs=[smem] + [vmem] * 3 + [hbm],
        out_specs=vmem,
        out_shape=block,
        scratch_shapes=[
            pltpu.VMEM((lat_count, lat_count), BF16),
            block_scratch,
            pltpu.VMEM((SHARE, XP, lat_count), BF16),
            pltpu.VMEM((SHARE, 2 * XP, lat_half), BF16),
            pltpu.VMEM((LEV, WIDE, RQ * count), F32),
            pltpu.VMEM((3,) + legendre.shape[1:], BF16),
            pltpu.SemaphoreType.DMA((3,)),
        ],
        compiler_params=params(54),
        name="spectral_round",
    )(places, arrived, rows_in, vert, legendre)
    returned = lax.all_to_all(solved, ("wave", "lev"), split_axis=0, concat_axis=0, tiled=True)
    restored = pl.pallas_call(
        restore_kernel,
        in_specs=[vmem] * 2,
        out_specs=hbm,
        out_shape=jax.ShapeDtypeStruct(rowed, BF16),
        scratch_shapes=[
            block_scratch,
            row_scratch,
            pltpu.VMEM(rowed, BF16),
            pltpu.SemaphoreType.DMA((RQ,)),
        ],
        compiler_params=params(48),
        name="restore_waves",
    )(wave_order, returned)
    restored = restored.reshape(2, LOCAL, RQ * R5, 2, waves)
    return restored.transpose(0, 3, 1, 2, 4)


def solution(mesh):
    placed = (
        P(None, None, "lev", "wave", None),
        P(),
        P(),
        P(),
        P("wave", None, None),
        P(),
        P(),
        P(),
        P(),
        P(),
        P(),
    )
    return jax.shard_map(
        local,
        mesh=mesh,
        in_specs=placed,
        out_specs=P(None, None, "lev", "wave", None),
        check_vma=False,
    )
```

```python
import jax
import jax.numpy as jnp
from jax import lax
from jax.experimental import pallas as pl
from jax.experimental.pallas import tpu as pltpu
from jax.sharding import PartitionSpec as P

RQ, R5 = 4, 5
ROWS = 8
PITCH = 40
LANES = 512
LEV = 4
LOCAL = 18
X = LEV * LOCAL
FL = 2 * LOCAL
UNIT = 40
XP = LEV * UNIT
PAIR = 2 * FL
XW = LEV * PAIR
SIDE = 384
HALF = 2 * SIDE
WIDE = 2 * LANES
TOTAL = 2 * XW + XP
WHOLE = ((0, 1), (3, 4), (5, 6), (8, 9))
SHARED = (2, 7)
CUTS = 2
NT = (((1,), (1,)), ((), ()))
TN = (((0,), (0,)), ((), ()))
NN = (((1,), (0,)), ((), ()))
F32 = jnp.float32
BF16 = jnp.bfloat16


def dot(a, b, dims):
    return lax.dot_general(a, b, dims, preferred_element_type=F32)


def params(mebibytes):
    return pltpu.CompilerParams(vmem_limit_bytes=mebibytes * 1024 * 1024)


def put_rows(scr, start, size, stride, values):
    width = scr.shape[2]
    for t in range(scr.shape[0]):
        scr[t, pl.ds(start, size, stride=stride), :] = values[:, t * width : (t + 1) * width]


def get_rows(scr, start, size, stride):
    tiles = [scr[t, pl.ds(start, size, stride=stride), :] for t in range(scr.shape[0])]
    return jnp.concatenate(tiles, axis=1)


def put_block(scr, block_ref):
    width = scr.shape[2]
    for w in range(block_ref.shape[0] // LEV):
        for t in range(scr.shape[0]):
            part = block_ref[w * LEV : (w + 1) * LEV, :, t * width : (t + 1) * width].astype(F32)
            scr[t, w * PITCH : w * PITCH + LEV * ROWS, :] = part.reshape(LEV * ROWS, width)


def get_block(scr, out_ref, first, last):
    width = scr.shape[2]
    for w in range(first, last):
        for t in range(scr.shape[0]):
            part = scr[t, w * PITCH : w * PITCH + LEV * ROWS, :].reshape(LEV, ROWS, width)
            out_ref[w * LEV : (w + 1) * LEV, :, t * width : (t + 1) * width] = part.astype(BF16)


def send_block(scr, out_buf, out_hbm, out_sem):
    peers = out_buf.shape[0] // LEV
    step = peers // CUTS
    stores = []
    for cut in range(CUTS):
        get_block(scr, out_buf, cut * step, (cut + 1) * step)
        part = pl.ds(cut * step * LEV, step * LEV)
        stores.append(pltpu.make_async_copy(out_buf.at[part], out_hbm.at[part], out_sem.at[cut]))
        stores[-1].start()
    for store in stores:
        store.wait()


def h_block(lat_half):
    return 128 if lat_half % 128 == 0 else lat_half


def wave_matrix(wave_ref, peers):
    count = wave_ref.shape[0]
    m_local = count // peers
    row = lax.broadcasted_iota(jnp.int32, (count, 1), 0)
    ids = lax.broadcasted_iota(jnp.int32, (count, count), 1)
    slot = lax.rem(row, peers) * m_local + lax.div(row, peers)
    waves = wave_ref[...].reshape(1, count).astype(F32)
    held = jnp.sum(jnp.where(ids == slot, waves, 0.0), axis=1, keepdims=True)
    return jnp.where(held == ids.astype(F32), 1.0, 0.0).astype(BF16)


def fill_lat_matrix(rows_ref, ot_scr):
    lat_count = ot_scr.shape[0]
    half = lat_count // 2
    hb = h_block(half)
    at = rows_ref.shape[0] - 3
    lats = jnp.concatenate([rows_ref[at : at + 1, :], rows_ref[at + 1 : at + 2, :]], axis=1)
    lats = lats.astype(jnp.int32)
    for block in range(half // hb):
        ids = lax.broadcasted_iota(jnp.int32, (hb, lat_count), 0) + block * hb
        north = jnp.where(lats == ids, 1.0, 0.0).astype(BF16)
        south = jnp.where(lats == lat_count - 1 - ids, 1.0, 0.0).astype(BF16)
        ot_scr[2 * block * hb : (2 * block + 1) * hb, :] = north
        ot_scr[(2 * block + 1) * hb : (2 * block + 2) * hb, :] = south


def part_matrix():
    row = lax.broadcasted_iota(jnp.int32, (SIDE, 2 * (WIDE - HALF)), 0)
    lane = lax.broadcasted_iota(jnp.int32, (1, 2 * (WIDE - HALF)), 1)
    c = lax.div(lane, WIDE - HALF)
    inner = lax.rem(lane, WIDE - HALF)
    unit, fl = lax.div(inner, UNIT), lax.rem(inner, UNIT)
    source = jnp.where((unit < R5) & (fl < FL), unit * PAIR + fl * 2 + c, -1)
    return jnp.where(row == source, 1.0, 0.0).astype(BF16)


def select_kernel(wave_ref, x_hbm, out_hbm, x_buf, z_scr, scr, out_buf, in_sem, out_sem):
    waves = z_scr.shape[2]
    peers = out_buf.shape[0] // LEV
    loads = []
    for rq in range(RQ):
        part = pl.ds(rq * R5, R5)
        loads.append(pltpu.make_async_copy(x_hbm.at[:, part], x_buf.at[:, part], in_sem.at[rq]))
        loads[-1].start()
    onehot = wave_matrix(wave_ref, peers)
    apart = part_matrix()
    z_scr[:, R5 * PAIR :, :] = jnp.zeros((RQ, SIDE - R5 * PAIR, waves), BF16)
    for rq in range(RQ):
        loads[rq].wait()
        for r5 in range(R5):
            piece = x_buf[:, rq * R5 + r5].reshape(PAIR, waves)
            z_scr[rq, r5 * PAIR : (r5 + 1) * PAIR, :] = piece
    for rq in range(RQ):
        got = dot(onehot, z_scr[rq], NT)

        def put(peer, tile, values):
            for t in range(values.shape[1] // 128):
                side, lane = (tile + t) // 4, (tile + t) % 4
                start = peer * ROWS + rq * 2 + side
                scr[lane, pl.ds(start, peers, stride=PITCH), :] = values[:, t * 128 : (t + 1) * 128]

        for peer in range(LEV):
            for i, kk in enumerate(WHOLE[peer]):
                put(peer, 3 * i, got[kk * peers : (kk + 1) * peers])
        both = jnp.concatenate([got[kk * peers : (kk + 1) * peers] for kk in SHARED], axis=0)
        both = dot(both.astype(BF16), apart, NN)
        for peer in range(LEV):
            rows = both[(peer // 2) * peers : (peer // 2 + 1) * peers]
            put(peer, 6, rows[:, (peer % 2) * (WIDE - HALF) : (peer % 2 + 1) * (WIDE - HALF)])
    send_block(scr, out_buf, out_hbm, out_sem)


def split(values):
    high = values.astype(BF16)
    return high, (values - high.astype(F32)).astype(BF16)


def slots_of(p):
    for i in range(2):
        yield i * SIDE, PAIR, i * XW + p * PAIR
    yield HALF, UNIT, 2 * XW + p * UNIT


def solve(state_low, factor, first, second, keep, modes):
    first_high, first_low = first
    second_high, second_low = second
    size = modes.shape[0]
    mixed = dot(first_high, state_low, NN) + dot(first_low, state_low, NN)
    modal = (mixed[:size] + factor * mixed[size:]) / (1.0 + factor * modes)
    modal_high, modal_low = split(modal)
    new = (
        dot(second_high, modal_high, NN)
        + dot(second_high, modal_low, NN)
        + dot(second_low, modal_high, NN)
    )
    return (new + keep * state_low.astype(F32)).astype(BF16)


def spectral_kernel(
    place_ref, r_ref, rows_ref, vert_ref, wide_ref, leg_hbm, out_ref,
    ot_scr, scr, lat_scr, sym_scr, anti_scr, band_scr, leg_buf, leg_sem,
):
    peers = r_ref.shape[0] // LEV
    half = ot_scr.shape[0] // 2
    hb = h_block(half)
    span = 2 * peers
    waves = rows_ref.shape[1]
    me = place_ref[place_ref.shape[0] - 1]
    whole = lax.div(5 * me + 1, 2)
    held = (whole, whole + 1, 2 + 5 * lax.div(me, 2))
    loads = []
    for i, kk in enumerate(held):
        loads.append(pltpu.make_async_copy(leg_hbm.at[kk], leg_buf.at[i], leg_sem.at[i]))
        loads[-1].start()
    fill_lat_matrix(rows_ref, ot_scr)
    put_block(scr, r_ref)
    for p in range(LEV):
        for pair in range(RQ // 2):
            part = jnp.concatenate(
                [
                    jnp.concatenate(
                        [get_rows(scr, p * ROWS + 2 * rq + side, peers, PITCH) for side in range(2)],
                        axis=1,
                    )
                    for rq in (2 * pair, 2 * pair + 1)
                ],
                axis=0,
            )
            turned = part.T
            for at, size, row in slots_of(p):
                for r5 in range(R5):
                    lane = (r5 * 2 + pair) * span
                    piece = turned[at + r5 * size : at + (r5 + 1) * size]
                    lat_scr[row : row + size, lane : lane + span] = piece.astype(BF16)
    lhs = lat_scr[...]
    for block in range(half // hb):
        both = dot(lhs, ot_scr[2 * block * hb : (2 * block + 2) * hb, :], NT)
        north, south = both[:, :hb], both[:, hb:]
        weight = rows_ref[rows_ref.shape[0] - 1 :, block * hb : (block + 1) * hb]
        sym_scr[:, block * hb : (block + 1) * hb] = ((north + south) * weight).astype(BF16)
        anti_scr[:, block * hb : (block + 1) * hb] = ((north - south) * weight).astype(BF16)

    wide = (
        split(wide_ref[:XW, :]),
        split(wide_ref[XW:, : 2 * X]),
        wide_ref[XW:, 2 * X : 2 * X + 1],
        wide_ref[XW : XW + 2 * X, 2 * X + 1 : 2 * X + 2],
    )
    narrow = (
        split(vert_ref[: 2 * X, :]),
        split(vert_ref[2 * X :, :X]),
        vert_ref[2 * X :, X : X + 1],
        vert_ref[2 * X : 3 * X, X + 1 : X + 2],
    )
    degree = lax.broadcasted_iota(jnp.int32, (1, waves), 1)
    factor = (degree * (degree + 1)).astype(F32) / float(waves * (waves + 1))
    for i, kk in enumerate(held):
        low, size = i * XW, XW if i < 2 else XP
        live = rows_ref[pl.ds(kk, 1), :]
        even = lax.rem(degree + place_ref[kk], 2) == 0
        loads[i].wait()
        leg = leg_buf[i]
        sym = dot(sym_scr[low : low + size, :], leg, NT)
        anti = dot(anti_scr[low : low + size, :], leg, NT)
        state_low = (jnp.where(even, sym, anti) * live).astype(BF16)
        new = solve(state_low, factor, *(wide if i < 2 else narrow)).astype(F32) * live
        signed = jnp.where(even, new, -new)
        north = dot(new.astype(BF16), leg, NN).astype(BF16)
        south = dot(signed.astype(BF16), leg, NN).astype(BF16)
        for block in range(half // hb):
            lane = 2 * block * hb
            lat_scr[low : low + size, lane : lane + hb] = north[:, block * hb : (block + 1) * hb]
            lat_scr[low : low + size, lane + hb : lane + 2 * hb] = south[:, block * hb : (block + 1) * hb]

    lhs = lat_scr[...]
    for r5 in range(R5):
        band = dot(lhs, ot_scr[:, 2 * r5 * span : 2 * (r5 + 1) * span], NN)
        for p in range(LEV):
            for at, size, row in slots_of(p):
                band_scr[p, at + r5 * size : at + (r5 + 1) * size, :] = band[row : row + size]
    for p in range(LEV):
        for pair in range(RQ // 2):
            turned = band_scr[p, :, pair * span : (pair + 1) * span].T
            for i in range(2):
                for side in range(2):
                    start = p * ROWS + (2 * pair + i) * 2 + side
                    piece = turned[i * peers : (i + 1) * peers, side * LANES : (side + 1) * LANES]
                    put_rows(scr, start, peers, PITCH, piece)
    get_block(scr, out_ref, 0, peers)


def restore_kernel(wave_ref, r_ref, out_hbm, scr, out_buf, out_sem):
    peers = r_ref.shape[0] // LEV
    waves = wave_ref.shape[0]
    onehot = wave_matrix(wave_ref, peers)
    apart = part_matrix()
    put_block(scr, r_ref)
    stores = []
    for rq in range(RQ):

        def get(peer, tile, tiles):
            values = []
            for t in range(tile, tile + tiles):
                start = peer * ROWS + rq * 2 + t // 4
                values.append(scr[t % 4, pl.ds(start, peers, stride=PITCH), :])
            return jnp.concatenate(values, axis=1)

        parts = {}
        for peer in range(LEV):
            for i, kk in enumerate(WHOLE[peer]):
                parts[kk] = get(peer, 3 * i, 3)
        lane = lax.broadcasted_iota(jnp.int32, (peers, WIDE - HALF), 1)
        shared = [
            jnp.concatenate(
                [jnp.where(lane < R5 * UNIT, get(2 * i + c, 6, 2), 0.0) for c in range(2)], axis=1
            )
            for i in range(2)
        ]
        shared = dot(jnp.concatenate(shared, axis=0).astype(BF16), apart, NT)
        for i, kk in enumerate(SHARED):
            parts[kk] = shared[i * peers : (i + 1) * peers]
        part = jnp.concatenate([parts[kk] for kk in sorted(parts)], axis=0).astype(BF16)
        got = dot(part, onehot, TN).astype(BF16)
        for r5 in range(R5):
            piece = got[r5 * PAIR : (r5 + 1) * PAIR].reshape(FL, 2, waves)
            out_buf[:, rq * R5 + r5] = piece
        part = pl.ds(rq * R5, R5)
        stores.append(pltpu.make_async_copy(out_buf.at[:, part], out_hbm.at[:, part], out_sem.at[rq]))
        stores[-1].start()
    for store in stores:
        store.wait()


def local(
    fourier,
    lat_order,
    wave_order,
    pattern,
    legendre,
    lat_weight,
    hydrostatic_thermal_link,
    evec,
    einv,
    spread_to_heat_link,
    modes,
):
    m_local, waves, lat_half = legendre.shape
    lat_count = 2 * lat_half
    count = waves // m_local
    block_count = pattern.shape[0]
    block_width = waves // block_count
    high = lax.Precision.HIGHEST

    lat_rows = lat_order.reshape(count, RQ, R5).transpose(2, 1, 0).reshape(2, lat_half).astype(F32)
    my_waves = lax.dynamic_slice_in_dim(wave_order, lax.axis_index("wave") * m_local, m_local)
    owner_rows = (
        my_waves[:, None] // block_width == jnp.arange(block_count, dtype=jnp.int32)[None, :]
    ).astype(F32)
    live_rows = jnp.dot(owner_rows, pattern.astype(F32), precision=high)
    live = jnp.repeat(live_rows, block_width, axis=1)
    rows_in = jnp.concatenate([live, lat_rows, lat_weight[None, :]], axis=0)
    places = jnp.concatenate([my_waves, lax.axis_index("lev")[None]]).astype(jnp.int32)

    einv_link = jnp.dot(einv, hydrostatic_thermal_link, precision=high)
    heat_evec = jnp.dot(spread_to_heat_link, evec, precision=high)
    gap = ((0, 0), (0, UNIT - FL), (0, 0))
    none = jnp.zeros((X, LEV, LOCAL), F32)
    tail = jnp.zeros((X, LEV, UNIT - FL), F32)
    first = jnp.concatenate(
        [
            jnp.concatenate([einv.reshape(X, LEV, LOCAL), none, tail], axis=2),
            jnp.concatenate([none, einv_link.reshape(X, LEV, LOCAL), tail], axis=2),
        ],
        axis=0,
    ).reshape(2 * X, XP)
    second = jnp.concatenate(
        [evec.reshape(LEV, LOCAL, X), -heat_evec.reshape(LEV, LOCAL, X)], axis=1
    )
    second = jnp.pad(second, gap).reshape(XP, X)
    place = jnp.arange(XP, dtype=jnp.int32) % UNIT
    keep = ((place >= LOCAL) & (place < FL)).astype(F32)[:, None]
    column = jnp.arange(XP, dtype=jnp.int32)[None, :]
    second = jnp.pad(second, ((0, 0), (0, XP - X))) + keep * (column == X).astype(F32)
    second = second + jnp.pad(modes, (0, XP - X))[:, None] * (column == X + 1).astype(F32)
    vert = jnp.concatenate([first, second], axis=0)

    twin = jnp.eye(2, dtype=F32)
    none = jnp.zeros((X, LEV, LOCAL), F32)
    fold = jnp.stack(
        [
            jnp.concatenate([einv.reshape(X, LEV, LOCAL), none], axis=2),
            jnp.concatenate([none, einv_link.reshape(X, LEV, LOCAL)], axis=2),
        ]
    ).reshape(2, X, 1, LEV, FL, 1)
    wide_first = (fold * twin.reshape(1, 1, 2, 1, 1, 2)).reshape(4 * X, XW)
    spread = jnp.concatenate(
        [evec.reshape(LEV, LOCAL, X), -heat_evec.reshape(LEV, LOCAL, X)], axis=1
    ).reshape(X * 2, 1, X, 1)
    wide_second = (spread * twin.reshape(1, 2, 1, 2)).reshape(XW, 2 * X)
    place = (jnp.arange(XW, dtype=jnp.int32) % PAIR) // 2
    keep = (place >= LOCAL).astype(F32)[:, None]
    column = jnp.arange(XW, dtype=jnp.int32)[None, :]
    wide_second = jnp.pad(wide_second, ((0, 0), (0, XW - 2 * X))) + keep * (column == 2 * X).astype(F32)
    modes_twin = jnp.pad(jnp.repeat(modes, 2), (0, XW - 2 * X))[:, None]
    wide_second = wide_second + modes_twin * (column == 2 * X + 1).astype(F32)
    wide_vert = jnp.concatenate([wide_first, wide_second], axis=0)

    vmem = pl.BlockSpec(memory_space=pltpu.VMEM)
    smem = pl.BlockSpec(memory_space=pltpu.SMEM)
    hbm = pl.BlockSpec(memory_space=pltpu.HBM)
    peers = count * LEV
    rowed = (FL, RQ * R5, 2, waves)
    block = jax.ShapeDtypeStruct((peers, ROWS, LANES), BF16)
    block_scratch = pltpu.VMEM((LANES // 128, count * PITCH, 128), F32)

    sent = pl.pallas_call(
        select_kernel,
        in_specs=[vmem, hbm],
        out_specs=hbm,
        out_shape=block,
        scratch_shapes=[
            pltpu.VMEM(rowed, BF16),
            pltpu.VMEM((RQ, SIDE, waves), BF16),
            block_scratch,
            pltpu.VMEM(block.shape, BF16),
            pltpu.SemaphoreType.DMA((RQ,)),
            pltpu.SemaphoreType.DMA((CUTS,)),
        ],
        compiler_params=params(60),
        name="select_waves",
    )(wave_order, fourier.transpose(0, 2, 3, 1, 4).reshape(rowed))
    arrived = lax.all_to_all(sent, ("wave", "lev"), split_axis=0, concat_axis=0, tiled=True)
    solved = pl.pallas_call(
        spectral_kernel,
        in_specs=[smem] + [vmem] * 4 + [hbm],
        out_specs=vmem,
        out_shape=block,
        scratch_shapes=[
            pltpu.VMEM((lat_count, lat_count), BF16),
            block_scratch,
            pltpu.VMEM((TOTAL, lat_count), BF16),
            pltpu.VMEM((TOTAL, lat_half), BF16),
            pltpu.VMEM((TOTAL, lat_half), BF16),
            pltpu.VMEM((LEV, WIDE, RQ * count), F32),
            pltpu.VMEM((3,) + legendre.shape[1:], BF16),
            pltpu.SemaphoreType.DMA((3,)),
        ],
        compiler_params=params(46),
        name="spectral_round",
    )(places, arrived, rows_in, vert, wide_vert, legendre)
    returned = lax.all_to_all(solved, ("wave", "lev"), split_axis=0, concat_axis=0, tiled=True)
    restored = pl.pallas_call(
        restore_kernel,
        in_specs=[vmem] * 2,
        out_specs=hbm,
        out_shape=jax.ShapeDtypeStruct(rowed, BF16),
        scratch_shapes=[
            block_scratch,
            pltpu.VMEM(rowed, BF16),
            pltpu.SemaphoreType.DMA((RQ,)),
        ],
        compiler_params=params(48),
        name="restore_waves",
    )(wave_order, returned)
    restored = restored.reshape(2, LOCAL, RQ * R5, 2, waves)
    return restored.transpose(0, 3, 1, 2, 4)


def solution(mesh):
    placed = (
        P(None, None, "lev", "wave", None),
        P(),
        P(),
        P(),
        P("wave", None, None),
        P(),
        P(),
        P(),
        P(),
        P(),
        P(),
    )
    return jax.shard_map(
        local,
        mesh=mesh,
        in_specs=placed,
        out_specs=P(None, None, "lev", "wave", None),
        check_vma=False,
    )
```

```python
import jax
import jax.numpy as jnp
from jax import lax
from jax.experimental import pallas as pl
from jax.experimental.pallas import tpu as pltpu
from jax.sharding import PartitionSpec as P

RQ, R5 = 4, 5
ROWS = 8
LANES = 512
LEV = 4
LOCAL = 18
X = LEV * LOCAL
FL = 2 * LOCAL
UNIT = 40
XP = LEV * UNIT
PAIR = 2 * FL
XW = LEV * PAIR
SIDE = 384
HALF = 2 * SIDE
WIDE = 2 * LANES
TOTAL = 2 * XW + XP
WHOLE = ((0, 1), (3, 4), (5, 6), (8, 9))
SHARED = (2, 7)
CUTS = 4
NT = (((1,), (1,)), ((), ()))
TN = (((0,), (0,)), ((), ()))
NN = (((1,), (0,)), ((), ()))
F32 = jnp.float32
BF16 = jnp.bfloat16


def dot(a, b, dims):
    return lax.dot_general(a, b, dims, preferred_element_type=F32)


def params(mebibytes):
    return pltpu.CompilerParams(vmem_limit_bytes=mebibytes * 1024 * 1024)


def put_rows(scr, start, size, stride, values):
    width = scr.shape[2]
    for t in range(scr.shape[0]):
        scr[t, pl.ds(start, size, stride=stride), :] = values[:, t * width : (t + 1) * width]


def get_rows(scr, start, size, stride):
    tiles = [scr[t, pl.ds(start, size, stride=stride), :] for t in range(scr.shape[0])]
    return jnp.concatenate(tiles, axis=1)


def put_block(scr, block_ref):
    width = scr.shape[2]
    for t in range(scr.shape[0]):
        part = block_ref[:, :, t * width : (t + 1) * width].astype(F32)
        scr[t] = part.reshape(scr.shape[1:])


def get_block(scr, out_ref, first, last):
    width = scr.shape[2]
    for t in range(scr.shape[0]):
        part = scr[t, first * ROWS : last * ROWS, :].reshape(last - first, ROWS, width)
        out_ref[first:last, :, t * width : (t + 1) * width] = part.astype(BF16)


def send_block(scr, out_buf, out_hbm, out_sem):
    step = out_buf.shape[0] // CUTS
    stores = []
    for cut in range(CUTS):
        get_block(scr, out_buf, cut * step, (cut + 1) * step)
        part = pl.ds(cut * step, step)
        stores.append(pltpu.make_async_copy(out_buf.at[part], out_hbm.at[part], out_sem.at[cut]))
        stores[-1].start()
    for store in stores:
        store.wait()


def h_block(lat_half):
    return 128 if lat_half % 128 == 0 else lat_half


def wave_matrix(wave_ref, peers):
    count = wave_ref.shape[0]
    m_local = count // peers
    row = lax.broadcasted_iota(jnp.int32, (count, 1), 0)
    ids = lax.broadcasted_iota(jnp.int32, (count, count), 1)
    slot = lax.rem(row, peers) * m_local + lax.div(row, peers)
    waves = wave_ref[...].reshape(1, count).astype(F32)
    held = jnp.sum(jnp.where(ids == slot, waves, 0.0), axis=1, keepdims=True)
    return jnp.where(held == ids.astype(F32), 1.0, 0.0).astype(BF16)


def fill_lat_matrix(rows_ref, ot_scr):
    lat_count = ot_scr.shape[0]
    half = lat_count // 2
    hb = h_block(half)
    at = rows_ref.shape[0] - 3
    lats = jnp.concatenate([rows_ref[at : at + 1, :], rows_ref[at + 1 : at + 2, :]], axis=1)
    lats = lats.astype(jnp.int32)
    for block in range(half // hb):
        ids = lax.broadcasted_iota(jnp.int32, (hb, lat_count), 0) + block * hb
        north = jnp.where(lats == ids, 1.0, 0.0).astype(BF16)
        south = jnp.where(lats == lat_count - 1 - ids, 1.0, 0.0).astype(BF16)
        ot_scr[2 * block * hb : (2 * block + 1) * hb, :] = north
        ot_scr[(2 * block + 1) * hb : (2 * block + 2) * hb, :] = south


def part_matrix():
    row = lax.broadcasted_iota(jnp.int32, (SIDE, 2 * (WIDE - HALF)), 0)
    lane = lax.broadcasted_iota(jnp.int32, (1, 2 * (WIDE - HALF)), 1)
    c = lax.div(lane, WIDE - HALF)
    inner = lax.rem(lane, WIDE - HALF)
    unit, fl = lax.div(inner, UNIT), lax.rem(inner, UNIT)
    source = jnp.where((unit < R5) & (fl < FL), unit * PAIR + fl * 2 + c, -1)
    return jnp.where(row == source, 1.0, 0.0).astype(BF16)


def select_kernel(wave_ref, x_hbm, out_hbm, x_buf, z_scr, scr, out_buf, in_sem, out_sem):
    waves = z_scr.shape[2]
    peers = out_buf.shape[0] // LEV
    loads = []
    for rq in range(RQ):
        part = pl.ds(rq * R5, R5)
        loads.append(pltpu.make_async_copy(x_hbm.at[:, part], x_buf.at[:, part], in_sem.at[rq]))
        loads[-1].start()
    onehot = wave_matrix(wave_ref, peers)
    apart = part_matrix()
    z_scr[:, R5 * PAIR :, :] = jnp.zeros((RQ, SIDE - R5 * PAIR, waves), BF16)
    for rq in range(RQ):
        loads[rq].wait()
        for r5 in range(R5):
            piece = x_buf[:, rq * R5 + r5].reshape(PAIR, waves)
            z_scr[rq, r5 * PAIR : (r5 + 1) * PAIR, :] = piece
    for rq in range(RQ):
        got = dot(onehot, z_scr[rq], NT)

        def put(peer, tile, values):
            for t in range(values.shape[1] // 128):
                side, lane = (tile + t) // 4, (tile + t) % 4
                start = peer * peers * ROWS + rq * 2 + side
                scr[lane, pl.ds(start, peers, stride=ROWS), :] = values[:, t * 128 : (t + 1) * 128]

        for peer in range(LEV):
            for i, kk in enumerate(WHOLE[peer]):
                put(peer, 3 * i, got[kk * peers : (kk + 1) * peers])
        both = jnp.concatenate([got[kk * peers : (kk + 1) * peers] for kk in SHARED], axis=0)
        both = dot(both.astype(BF16), apart, NN)
        for peer in range(LEV):
            rows = both[(peer // 2) * peers : (peer // 2 + 1) * peers]
            put(peer, 6, rows[:, (peer % 2) * (WIDE - HALF) : (peer % 2 + 1) * (WIDE - HALF)])
    send_block(scr, out_buf, out_hbm, out_sem)


def slots_of(p):
    for i in range(2):
        yield i * SIDE, PAIR, i * XW + p * PAIR
    yield HALF, UNIT, 2 * XW + p * UNIT


def solve(state_low, factor, first, second, keep, modes):
    size = modes.shape[0]
    mixed = dot(first, jnp.concatenate([state_low, state_low], axis=0), NN)
    modal = (mixed[:size] + factor * mixed[size:]) / (1.0 + factor * modes)
    high = modal.astype(BF16).astype(F32)
    stacked = jnp.concatenate([high, modal - high, high], axis=0).astype(BF16)
    new = dot(second, stacked, NN)
    return (new + keep * state_low.astype(F32)).astype(BF16)


def spectral_kernel(
    place_ref, r_ref, rows_ref, vert_ref, wide_ref, leg_hbm, out_ref,
    ot_scr, scr, lat_scr, sym_scr, anti_scr, band_scr, leg_buf, leg_sem,
):
    peers = r_ref.shape[0] // LEV
    half = ot_scr.shape[0] // 2
    hb = h_block(half)
    span = 2 * peers
    waves = rows_ref.shape[1]
    me = place_ref[place_ref.shape[0] - 1]
    whole = lax.div(5 * me + 1, 2)
    held = (whole, whole + 1, 2 + 5 * lax.div(me, 2))
    loads = []
    for i, kk in enumerate(held):
        loads.append(pltpu.make_async_copy(leg_hbm.at[kk], leg_buf.at[i], leg_sem.at[i]))
        loads[-1].start()
    fill_lat_matrix(rows_ref, ot_scr)
    put_block(scr, r_ref)
    for p in range(LEV):
        for pair in range(RQ // 2):
            part = jnp.concatenate(
                [
                    jnp.concatenate(
                        [get_rows(scr, p * peers * ROWS + 2 * rq + side, peers, ROWS) for side in range(2)],
                        axis=1,
                    )
                    for rq in (2 * pair, 2 * pair + 1)
                ],
                axis=0,
            )
            turned = part.T
            for at, size, row in slots_of(p):
                for r5 in range(R5):
                    lane = (r5 * 2 + pair) * span
                    piece = turned[at + r5 * size : at + (r5 + 1) * size]
                    lat_scr[row : row + size, lane : lane + span] = piece.astype(BF16)
    lhs = lat_scr[...]
    for block in range(half // hb):
        both = dot(lhs, ot_scr[2 * block * hb : (2 * block + 2) * hb, :], NT)
        north, south = both[:, :hb], both[:, hb:]
        weight = rows_ref[rows_ref.shape[0] - 1 :, block * hb : (block + 1) * hb]
        sym_scr[:, block * hb : (block + 1) * hb] = ((north + south) * weight).astype(BF16)
        anti_scr[:, block * hb : (block + 1) * hb] = ((north - south) * weight).astype(BF16)

    wide, narrow = (
        (
            ref[: 2 * size, : 2 * span_in].astype(BF16),
            ref[2 * size :, : 3 * size].astype(BF16),
            ref[2 * size :, 3 * size : 3 * size + 1],
            ref[2 * size : 3 * size, 3 * size + 1 : 3 * size + 2],
        )
        for ref, size, span_in in ((wide_ref, 2 * X, XW), (vert_ref, X, XP))
    )
    degree = lax.broadcasted_iota(jnp.int32, (1, waves), 1)
    factor = (degree * (degree + 1)).astype(F32) / float(waves * (waves + 1))
    for i, kk in enumerate(held):
        low, size = i * XW, XW if i < 2 else XP
        live = rows_ref[pl.ds(kk, 1), :]
        even = lax.rem(degree + place_ref[kk], 2) == 0
        loads[i].wait()
        leg = leg_buf[i]
        sym = dot(sym_scr[low : low + size, :], leg, NT)
        anti = dot(anti_scr[low : low + size, :], leg, NT)
        state_low = (jnp.where(even, sym, anti) * live).astype(BF16)
        new = solve(state_low, factor, *(wide if i < 2 else narrow)).astype(F32) * live
        signed = jnp.where(even, new, -new)
        north = dot(new.astype(BF16), leg, NN).astype(BF16)
        south = dot(signed.astype(BF16), leg, NN).astype(BF16)
        for block in range(half // hb):
            lane = 2 * block * hb
            lat_scr[low : low + size, lane : lane + hb] = north[:, block * hb : (block + 1) * hb]
            lat_scr[low : low + size, lane + hb : lane + 2 * hb] = south[:, block * hb : (block + 1) * hb]

    lhs = lat_scr[...]
    for r5 in range(R5):
        band = dot(lhs, ot_scr[:, 2 * r5 * span : 2 * (r5 + 1) * span], NN)
        for p in range(LEV):
            for at, size, row in slots_of(p):
                band_scr[p, at + r5 * size : at + (r5 + 1) * size, :] = band[row : row + size]
    for p in range(LEV):
        for pair in range(RQ // 2):
            turned = band_scr[p, :, pair * span : (pair + 1) * span].T
            for i in range(2):
                for side in range(2):
                    start = p * peers * ROWS + (2 * pair + i) * 2 + side
                    piece = turned[i * peers : (i + 1) * peers, side * LANES : (side + 1) * LANES]
                    put_rows(scr, start, peers, ROWS, piece)
    get_block(scr, out_ref, 0, out_ref.shape[0])


def restore_kernel(wave_ref, r_ref, out_hbm, scr, out_buf, out_sem):
    peers = r_ref.shape[0] // LEV
    waves = wave_ref.shape[0]
    onehot = wave_matrix(wave_ref, peers)
    apart = part_matrix()
    put_block(scr, r_ref)
    stores = []
    for rq in range(RQ):

        def get(peer, tile, tiles):
            values = []
            for t in range(tile, tile + tiles):
                start = peer * peers * ROWS + rq * 2 + t // 4
                values.append(scr[t % 4, pl.ds(start, peers, stride=ROWS), :])
            return jnp.concatenate(values, axis=1)

        parts = {}
        for peer in range(LEV):
            for i, kk in enumerate(WHOLE[peer]):
                parts[kk] = get(peer, 3 * i, 3)
        lane = lax.broadcasted_iota(jnp.int32, (peers, WIDE - HALF), 1)
        shared = [
            jnp.concatenate(
                [jnp.where(lane < R5 * UNIT, get(2 * i + c, 6, 2), 0.0) for c in range(2)], axis=1
            )
            for i in range(2)
        ]
        shared = dot(jnp.concatenate(shared, axis=0).astype(BF16), apart, NT)
        for i, kk in enumerate(SHARED):
            parts[kk] = shared[i * peers : (i + 1) * peers]
        part = jnp.concatenate([parts[kk] for kk in sorted(parts)], axis=0).astype(BF16)
        got = dot(part, onehot, TN).astype(BF16)
        for r5 in range(R5):
            piece = got[r5 * PAIR : (r5 + 1) * PAIR].reshape(FL, 2, waves)
            out_buf[:, rq * R5 + r5] = piece
        part = pl.ds(rq * R5, R5)
        stores.append(pltpu.make_async_copy(out_buf.at[:, part], out_hbm.at[:, part], out_sem.at[rq]))
        stores[-1].start()
    for store in stores:
        store.wait()


def stack_terms(first, second, keep, modes):
    def parts(matrix):
        high = lax.reduce_precision(matrix, 8, 7)
        return high, matrix - high

    first_high, first_low = parts(first)
    second_high, second_low = parts(second)
    rows, size = second.shape
    column = jnp.pad(modes, (0, rows - size))[:, None]
    top = jnp.concatenate([first_high, first_low], axis=1)
    bottom = jnp.concatenate([second_high, second_high, second_low, keep, column], axis=1)
    bottom = jnp.pad(bottom, ((0, 0), (0, top.shape[1] - bottom.shape[1])))
    return jnp.concatenate([top, bottom], axis=0)


def local(
    fourier,
    lat_order,
    wave_order,
    pattern,
    legendre,
    lat_weight,
    hydrostatic_thermal_link,
    evec,
    einv,
    spread_to_heat_link,
    modes,
):
    m_local, waves, lat_half = legendre.shape
    lat_count = 2 * lat_half
    count = waves // m_local
    block_count = pattern.shape[0]
    block_width = waves // block_count
    high = lax.Precision.HIGHEST

    lat_rows = lat_order.reshape(count, RQ, R5).transpose(2, 1, 0).reshape(2, lat_half).astype(F32)
    my_waves = lax.dynamic_slice_in_dim(wave_order, lax.axis_index("wave") * m_local, m_local)
    owner_rows = (
        my_waves[:, None] // block_width == jnp.arange(block_count, dtype=jnp.int32)[None, :]
    ).astype(F32)
    live_rows = jnp.dot(owner_rows, pattern.astype(F32), precision=high)
    live = jnp.repeat(live_rows, block_width, axis=1)
    rows_in = jnp.concatenate([live, lat_rows, lat_weight[None, :]], axis=0)
    places = jnp.concatenate([my_waves, lax.axis_index("lev")[None]]).astype(jnp.int32)

    einv_link = jnp.dot(einv, hydrostatic_thermal_link, precision=high)
    heat_evec = jnp.dot(spread_to_heat_link, evec, precision=high)
    gap = ((0, 0), (0, UNIT - FL), (0, 0))
    none = jnp.zeros((X, LEV, LOCAL), F32)
    tail = jnp.zeros((X, LEV, UNIT - FL), F32)
    first = jnp.concatenate(
        [
            jnp.concatenate([einv.reshape(X, LEV, LOCAL), none, tail], axis=2),
            jnp.concatenate([none, einv_link.reshape(X, LEV, LOCAL), tail], axis=2),
        ],
        axis=0,
    ).reshape(2 * X, XP)
    second = jnp.concatenate(
        [evec.reshape(LEV, LOCAL, X), -heat_evec.reshape(LEV, LOCAL, X)], axis=1
    )
    second = jnp.pad(second, gap).reshape(XP, X)
    place = jnp.arange(XP, dtype=jnp.int32) % UNIT
    keep = ((place >= LOCAL) & (place < FL)).astype(F32)[:, None]
    vert = stack_terms(first, second, keep, modes)

    twin = jnp.eye(2, dtype=F32)
    none = jnp.zeros((X, LEV, LOCAL), F32)
    fold = jnp.stack(
        [
            jnp.concatenate([einv.reshape(X, LEV, LOCAL), none], axis=2),
            jnp.concatenate([none, einv_link.reshape(X, LEV, LOCAL)], axis=2),
        ]
    ).reshape(2, X, 1, LEV, FL, 1)
    wide_first = (fold * twin.reshape(1, 1, 2, 1, 1, 2)).reshape(4 * X, XW)
    spread = jnp.concatenate(
        [evec.reshape(LEV, LOCAL, X), -heat_evec.reshape(LEV, LOCAL, X)], axis=1
    ).reshape(X * 2, 1, X, 1)
    wide_second = (spread * twin.reshape(1, 2, 1, 2)).reshape(XW, 2 * X)
    place = (jnp.arange(XW, dtype=jnp.int32) % PAIR) // 2
    keep = (place >= LOCAL).astype(F32)[:, None]
    wide_vert = stack_terms(wide_first, wide_second, keep, jnp.repeat(modes, 2))

    vmem = pl.BlockSpec(memory_space=pltpu.VMEM)
    smem = pl.BlockSpec(memory_space=pltpu.SMEM)
    hbm = pl.BlockSpec(memory_space=pltpu.HBM)
    peers = count * LEV
    rowed = (FL, RQ * R5, 2, waves)
    block = jax.ShapeDtypeStruct((peers, ROWS, LANES), BF16)
    block_scratch = pltpu.VMEM((LANES // 128, peers * ROWS, 128), F32)

    sent = pl.pallas_call(
        select_kernel,
        in_specs=[vmem, hbm],
        out_specs=hbm,
        out_shape=block,
        scratch_shapes=[
            pltpu.VMEM(rowed, BF16),
            pltpu.VMEM((RQ, SIDE, waves), BF16),
            block_scratch,
            pltpu.VMEM(block.shape, BF16),
            pltpu.SemaphoreType.DMA((RQ,)),
            pltpu.SemaphoreType.DMA((CUTS,)),
        ],
        compiler_params=params(60),
        name="select_waves",
    )(wave_order, fourier.transpose(0, 2, 3, 1, 4).reshape(rowed))
    arrived = lax.all_to_all(sent, ("lev", "wave"), split_axis=0, concat_axis=0, tiled=True)
    solved = pl.pallas_call(
        spectral_kernel,
        in_specs=[smem] + [vmem] * 4 + [hbm],
        out_specs=vmem,
        out_shape=block,
        scratch_shapes=[
            pltpu.VMEM((lat_count, lat_count), BF16),
            block_scratch,
            pltpu.VMEM((TOTAL, lat_count), BF16),
            pltpu.VMEM((TOTAL, lat_half), BF16),
            pltpu.VMEM((TOTAL, lat_half), BF16),
            pltpu.VMEM((LEV, WIDE, RQ * count), F32),
            pltpu.VMEM((3,) + legendre.shape[1:], BF16),
            pltpu.SemaphoreType.DMA((3,)),
        ],
        compiler_params=params(46),
        name="spectral_round",
    )(places, arrived, rows_in, vert, wide_vert, legendre)
    returned = lax.all_to_all(solved, ("lev", "wave"), split_axis=0, concat_axis=0, tiled=True)
    restored = pl.pallas_call(
        restore_kernel,
        in_specs=[vmem] * 2,
        out_specs=hbm,
        out_shape=jax.ShapeDtypeStruct(rowed, BF16),
        scratch_shapes=[
            block_scratch,
            pltpu.VMEM(rowed, BF16),
            pltpu.SemaphoreType.DMA((RQ,)),
        ],
        compiler_params=params(48),
        name="restore_waves",
    )(wave_order, returned)
    restored = restored.reshape(2, LOCAL, RQ * R5, 2, waves)
    return restored.transpose(0, 3, 1, 2, 4)


def solution(mesh):
    placed = (
        P(None, None, "lev", "wave", None),
        P(),
        P(),
        P(),
        P("wave", None, None),
        P(),
        P(),
        P(),
        P(),
        P(),
        P(),
    )
    return jax.shard_map(
        local,
        mesh=mesh,
        in_specs=placed,
        out_specs=P(None, None, "lev", "wave", None),
        check_vma=False,
    )
```

```python
import jax
import jax.numpy as jnp
from jax import lax
from jax.experimental import pallas as pl
from jax.experimental.pallas import tpu as pltpu
from jax.sharding import PartitionSpec as P

RQ, R5 = 4, 5
ROWS = 8
LANES = 512
LEV = 4
LOCAL = 18
X = LEV * LOCAL
FL = 2 * LOCAL
UNIT = 40
XP = LEV * UNIT
PAIR = 2 * FL
XW = LEV * PAIR
SIDE = 384
HALF = 2 * SIDE
WIDE = 2 * LANES
TOTAL = 2 * XW + XP
WHOLE = ((0, 1), (3, 4), (5, 6), (8, 9))
SHARED = (2, 7)
CUTS = 4
NT = (((1,), (1,)), ((), ()))
TN = (((0,), (0,)), ((), ()))
NN = (((1,), (0,)), ((), ()))
F32 = jnp.float32
BF16 = jnp.bfloat16


def dot(a, b, dims):
    return lax.dot_general(a, b, dims, preferred_element_type=F32)


def params(mebibytes):
    return pltpu.CompilerParams(vmem_limit_bytes=mebibytes * 1024 * 1024)


def put_rows(scr, start, size, stride, values):
    width = scr.shape[2]
    for t in range(scr.shape[0]):
        scr[t, pl.ds(start, size, stride=stride), :] = values[:, t * width : (t + 1) * width]


def get_rows(scr, start, size, stride):
    tiles = [scr[t, pl.ds(start, size, stride=stride), :] for t in range(scr.shape[0])]
    return jnp.concatenate(tiles, axis=1)


def put_block(scr, block_ref):
    width = scr.shape[2]
    for t in range(scr.shape[0]):
        part = block_ref[:, :, t * width : (t + 1) * width].astype(F32)
        scr[t] = part.reshape(scr.shape[1:])


def get_block(scr, out_ref, first, last):
    width = scr.shape[2]
    for t in range(scr.shape[0]):
        part = scr[t, first * ROWS : last * ROWS, :].reshape(last - first, ROWS, width)
        out_ref[first:last, :, t * width : (t + 1) * width] = part.astype(BF16)


def send_block(scr, out_buf, out_hbm, out_sem):
    step = out_buf.shape[0] // CUTS
    stores = []
    for cut in range(CUTS):
        get_block(scr, out_buf, cut * step, (cut + 1) * step)
        part = pl.ds(cut * step, step)
        stores.append(pltpu.make_async_copy(out_buf.at[part], out_hbm.at[part], out_sem.at[cut]))
        stores[-1].start()
    for store in stores:
        store.wait()


def h_block(lat_half):
    return 128 if lat_half % 128 == 0 else lat_half


def wave_matrix(wave_ref, peers):
    count = wave_ref.shape[0]
    m_local = count // peers
    row = lax.broadcasted_iota(jnp.int32, (count, 1), 0)
    ids = lax.broadcasted_iota(jnp.int32, (count, count), 1)
    slot = lax.rem(row, peers) * m_local + lax.div(row, peers)
    waves = wave_ref[...].reshape(1, count).astype(F32)
    held = jnp.sum(jnp.where(ids == slot, waves, 0.0), axis=1, keepdims=True)
    return jnp.where(held == ids.astype(F32), 1.0, 0.0).astype(BF16)


def fill_lat_matrix(rows_ref, ot_scr):
    lat_count = ot_scr.shape[0]
    half = lat_count // 2
    hb = h_block(half)
    at = rows_ref.shape[0] - 3
    lats = jnp.concatenate([rows_ref[at : at + 1, :], rows_ref[at + 1 : at + 2, :]], axis=1)
    lats = lats.astype(jnp.int32)
    for block in range(half // hb):
        ids = lax.broadcasted_iota(jnp.int32, (hb, lat_count), 0) + block * hb
        north = jnp.where(lats == ids, 1.0, 0.0).astype(BF16)
        south = jnp.where(lats == lat_count - 1 - ids, 1.0, 0.0).astype(BF16)
        ot_scr[2 * block * hb : (2 * block + 1) * hb, :] = north
        ot_scr[(2 * block + 1) * hb : (2 * block + 2) * hb, :] = south


def part_matrix():
    row = lax.broadcasted_iota(jnp.int32, (SIDE, 2 * (WIDE - HALF)), 0)
    lane = lax.broadcasted_iota(jnp.int32, (1, 2 * (WIDE - HALF)), 1)
    c = lax.div(lane, WIDE - HALF)
    inner = lax.rem(lane, WIDE - HALF)
    unit, fl = lax.div(inner, UNIT), lax.rem(inner, UNIT)
    source = jnp.where((unit < R5) & (fl < FL), unit * PAIR + fl * 2 + c, -1)
    return jnp.where(row == source, 1.0, 0.0).astype(BF16)


def select_kernel(wave_ref, x_hbm, out_hbm, x_buf, z_scr, scr, out_buf, in_sem, out_sem):
    waves = z_scr.shape[2]
    peers = out_buf.shape[0] // LEV
    loads = []
    for rq in range(RQ):
        part = pl.ds(rq * R5, R5)
        loads.append(pltpu.make_async_copy(x_hbm.at[:, part], x_buf.at[:, part], in_sem.at[rq]))
        loads[-1].start()
    onehot = wave_matrix(wave_ref, peers)
    apart = part_matrix()
    z_scr[:, R5 * PAIR :, :] = jnp.zeros((RQ, SIDE - R5 * PAIR, waves), BF16)
    for rq in range(RQ):
        loads[rq].wait()
        for r5 in range(R5):
            piece = x_buf[:, rq * R5 + r5].reshape(PAIR, waves)
            z_scr[rq, r5 * PAIR : (r5 + 1) * PAIR, :] = piece
    for rq in range(RQ):
        got = dot(onehot, z_scr[rq], NT)

        def put(peer, tile, values):
            for t in range(values.shape[1] // 128):
                side, lane = (tile + t) // 4, (tile + t) % 4
                start = peer * peers * ROWS + rq * 2 + side
                scr[lane, pl.ds(start, peers, stride=ROWS), :] = values[:, t * 128 : (t + 1) * 128]

        for peer in range(LEV):
            for i, kk in enumerate(WHOLE[peer]):
                put(peer, 3 * i, got[kk * peers : (kk + 1) * peers])
        both = jnp.concatenate([got[kk * peers : (kk + 1) * peers] for kk in SHARED], axis=0)
        both = dot(both.astype(BF16), apart, NN)
        for peer in range(LEV):
            rows = both[(peer // 2) * peers : (peer // 2 + 1) * peers]
            put(peer, 6, rows[:, (peer % 2) * (WIDE - HALF) : (peer % 2 + 1) * (WIDE - HALF)])
    send_block(scr, out_buf, out_hbm, out_sem)


def slots_of(p):
    for i in range(2):
        yield i * SIDE, PAIR, i * XW + p * PAIR
    yield HALF, UNIT, 2 * XW + p * UNIT


def solve(state_low, factor, first, second, keep, modes):
    size = modes.shape[0]
    mixed = dot(first, jnp.concatenate([state_low, state_low], axis=0), NN)
    modal = (mixed[:size] + factor * mixed[size:]) / (1.0 + factor * modes)
    high = modal.astype(BF16).astype(F32)
    stacked = jnp.concatenate([high, modal - high, high], axis=0).astype(BF16)
    new = dot(second, stacked, NN)
    return (new + keep * state_low.astype(F32)).astype(BF16)


def spectral_kernel(
    place_ref, r_ref, rows_ref, vert_ref, wide_ref, leg_hbm, out_ref,
    ot_scr, scr, lat_scr, sym_scr, anti_scr, band_scr, leg_buf, leg_sem,
):
    peers = r_ref.shape[0] // LEV
    half = ot_scr.shape[0] // 2
    hb = h_block(half)
    span = 2 * peers
    waves = rows_ref.shape[1]
    me = place_ref[place_ref.shape[0] - 1]
    whole = lax.div(5 * me + 1, 2)
    held = (whole, whole + 1, 2 + 5 * lax.div(me, 2))
    loads = []
    for i, kk in enumerate(held):
        loads.append(pltpu.make_async_copy(leg_hbm.at[kk], leg_buf.at[i], leg_sem.at[i]))
        loads[-1].start()
    fill_lat_matrix(rows_ref, ot_scr)
    put_block(scr, r_ref)
    for p in range(LEV):
        for pair in range(RQ // 2):
            part = jnp.concatenate(
                [
                    jnp.concatenate(
                        [get_rows(scr, p * peers * ROWS + 2 * rq + side, peers, ROWS) for side in range(2)],
                        axis=1,
                    )
                    for rq in (2 * pair, 2 * pair + 1)
                ],
                axis=0,
            )
            turned = part.T
            for at, size, row in slots_of(p):
                for r5 in range(R5):
                    lane = (r5 * 2 + pair) * span
                    piece = turned[at + r5 * size : at + (r5 + 1) * size]
                    lat_scr[row : row + size, lane : lane + span] = piece.astype(BF16)
    lhs = lat_scr[...]
    for block in range(half // hb):
        both = dot(lhs, ot_scr[2 * block * hb : (2 * block + 2) * hb, :], NT)
        north, south = both[:, :hb], both[:, hb:]
        weight = rows_ref[rows_ref.shape[0] - 1 :, block * hb : (block + 1) * hb]
        sym_scr[:, block * hb : (block + 1) * hb] = ((north + south) * weight).astype(BF16)
        anti_scr[:, block * hb : (block + 1) * hb] = ((north - south) * weight).astype(BF16)

    wide, narrow = (
        (
            ref[: 2 * size, : 2 * span_in].astype(BF16),
            ref[2 * size :, : 3 * size].astype(BF16),
            ref[2 * size :, 3 * size : 3 * size + 1],
            ref[2 * size : 3 * size, 3 * size + 1 : 3 * size + 2],
        )
        for ref, size, span_in in ((wide_ref, 2 * X, XW), (vert_ref, X, XP))
    )
    degree = lax.broadcasted_iota(jnp.int32, (1, waves), 1)
    factor = (degree * (degree + 1)).astype(F32) / float(waves * (waves + 1))
    for i, kk in enumerate(held):
        low, size = i * XW, XW if i < 2 else XP
        live = rows_ref[pl.ds(kk, 1), :]
        even = lax.rem(degree + place_ref[kk], 2) == 0
        loads[i].wait()
        leg = leg_buf[i]
        sym = dot(sym_scr[low : low + size, :], leg, NT)
        anti = dot(anti_scr[low : low + size, :], leg, NT)
        state_low = (jnp.where(even, sym, anti) * live).astype(BF16)
        new = solve(state_low, factor, *(wide if i < 2 else narrow)).astype(F32) * live
        signed = jnp.where(even, new, -new)
        north = dot(new.astype(BF16), leg, NN).astype(BF16)
        south = dot(signed.astype(BF16), leg, NN).astype(BF16)
        for block in range(half // hb):
            lane = 2 * block * hb
            lat_scr[low : low + size, lane : lane + hb] = north[:, block * hb : (block + 1) * hb]
            lat_scr[low : low + size, lane + hb : lane + 2 * hb] = south[:, block * hb : (block + 1) * hb]

    lhs = lat_scr[...]
    for r5 in range(R5):
        band = dot(lhs, ot_scr[:, 2 * r5 * span : 2 * (r5 + 1) * span], NN)
        for p in range(LEV):
            for at, size, row in slots_of(p):
                band_scr[p, at + r5 * size : at + (r5 + 1) * size, :] = band[row : row + size]
    for p in range(LEV):
        for pair in range(RQ // 2):
            turned = band_scr[p, :, pair * span : (pair + 1) * span].T
            for i in range(2):
                for side in range(2):
                    start = p * peers * ROWS + (2 * pair + i) * 2 + side
                    piece = turned[i * peers : (i + 1) * peers, side * LANES : (side + 1) * LANES]
                    put_rows(scr, start, peers, ROWS, piece)
    get_block(scr, out_ref, 0, out_ref.shape[0])


def restore_kernel(wave_ref, r_ref, out_hbm, scr, out_buf, out_sem):
    peers = r_ref.shape[0] // LEV
    waves = wave_ref.shape[0]
    onehot = wave_matrix(wave_ref, peers)
    apart = part_matrix()
    put_block(scr, r_ref)
    stores = []
    for rq in range(RQ):

        def get(peer, tile, tiles):
            values = []
            for t in range(tile, tile + tiles):
                start = peer * peers * ROWS + rq * 2 + t // 4
                values.append(scr[t % 4, pl.ds(start, peers, stride=ROWS), :])
            return jnp.concatenate(values, axis=1)

        parts = {}
        for peer in range(LEV):
            for i, kk in enumerate(WHOLE[peer]):
                parts[kk] = get(peer, 3 * i, 3)
        lane = lax.broadcasted_iota(jnp.int32, (peers, WIDE - HALF), 1)
        shared = [
            jnp.concatenate(
                [jnp.where(lane < R5 * UNIT, get(2 * i + c, 6, 2), 0.0) for c in range(2)], axis=1
            )
            for i in range(2)
        ]
        shared = dot(jnp.concatenate(shared, axis=0).astype(BF16), apart, NT)
        for i, kk in enumerate(SHARED):
            parts[kk] = shared[i * peers : (i + 1) * peers]
        part = jnp.concatenate([parts[kk] for kk in sorted(parts)], axis=0).astype(BF16)
        got = dot(part, onehot, TN).astype(BF16)
        for r5 in range(R5):
            piece = got[r5 * PAIR : (r5 + 1) * PAIR].reshape(FL, 2, waves)
            out_buf[:, rq * R5 + r5] = piece
        part = pl.ds(rq * R5, R5)
        stores.append(pltpu.make_async_copy(out_buf.at[:, part], out_hbm.at[:, part], out_sem.at[rq]))
        stores[-1].start()
    for store in stores:
        store.wait()


def stack_terms(first, second, keep, modes):
    def parts(matrix):
        high = lax.reduce_precision(matrix, 8, 7)
        return high, matrix - high

    first_high, first_low = parts(first)
    second_high, second_low = parts(second)
    rows, size = second.shape
    column = jnp.pad(modes, (0, rows - size))[:, None]
    top = jnp.concatenate([first_high, first_low], axis=1)
    bottom = jnp.concatenate([second_high, second_high, second_low, keep, column], axis=1)
    bottom = jnp.pad(bottom, ((0, 0), (0, top.shape[1] - bottom.shape[1])))
    return jnp.concatenate([top, bottom], axis=0)


def local(
    fourier,
    lat_order,
    wave_order,
    pattern,
    legendre,
    lat_weight,
    hydrostatic_thermal_link,
    evec,
    einv,
    spread_to_heat_link,
    modes,
):
    m_local, waves, lat_half = legendre.shape
    lat_count = 2 * lat_half
    count = waves // m_local
    block_count = pattern.shape[0]
    block_width = waves // block_count
    high = lax.Precision.HIGHEST

    lat_rows = lat_order.reshape(count, RQ, R5).transpose(2, 1, 0).reshape(2, lat_half).astype(F32)
    my_waves = lax.dynamic_slice_in_dim(wave_order, lax.axis_index("wave") * m_local, m_local)
    owner_rows = (
        my_waves[:, None] // block_width == jnp.arange(block_count, dtype=jnp.int32)[None, :]
    ).astype(F32)
    live_rows = jnp.dot(owner_rows, pattern.astype(F32), precision=high)
    live = jnp.repeat(live_rows, block_width, axis=1)
    rows_in = jnp.concatenate([live, lat_rows, lat_weight[None, :]], axis=0)
    places = jnp.concatenate([my_waves, lax.axis_index("lev")[None]]).astype(jnp.int32)

    einv_link = jnp.dot(einv, hydrostatic_thermal_link, precision=high)
    heat_evec = jnp.dot(spread_to_heat_link, evec, precision=high)
    gap = ((0, 0), (0, UNIT - FL), (0, 0))
    none = jnp.zeros((X, LEV, LOCAL), F32)
    tail = jnp.zeros((X, LEV, UNIT - FL), F32)
    first = jnp.concatenate(
        [
            jnp.concatenate([einv.reshape(X, LEV, LOCAL), none, tail], axis=2),
            jnp.concatenate([none, einv_link.reshape(X, LEV, LOCAL), tail], axis=2),
        ],
        axis=0,
    ).reshape(2 * X, XP)
    second = jnp.concatenate(
        [evec.reshape(LEV, LOCAL, X), -heat_evec.reshape(LEV, LOCAL, X)], axis=1
    )
    second = jnp.pad(second, gap).reshape(XP, X)
    place = jnp.arange(XP, dtype=jnp.int32) % UNIT
    keep = ((place >= LOCAL) & (place < FL)).astype(F32)[:, None]
    vert = stack_terms(first, second, keep, modes)

    def twin(matrix):
        rows, columns = matrix.shape
        down = jnp.arange(2 * rows, dtype=jnp.int32)[:, None]
        across = jnp.arange(2 * columns, dtype=jnp.int32)[None, :]
        left = (down // 2 == jnp.arange(rows, dtype=jnp.int32)[None, :]).astype(F32)
        right = (across // 2 == jnp.arange(columns, dtype=jnp.int32)[:, None]).astype(F32)
        spread = jnp.dot(jnp.dot(left, matrix, precision=high), right, precision=high)
        return jnp.where(down % 2 == across % 2, spread, 0.0)

    none = jnp.zeros((X, LEV, LOCAL), F32)
    fold = jnp.stack(
        [
            jnp.concatenate([einv.reshape(X, LEV, LOCAL), none], axis=2),
            jnp.concatenate([none, einv_link.reshape(X, LEV, LOCAL)], axis=2),
        ]
    ).reshape(2 * X, 2 * X)
    wide_first = twin(fold)
    spread = jnp.concatenate(
        [evec.reshape(LEV, LOCAL, X), -heat_evec.reshape(LEV, LOCAL, X)], axis=1
    ).reshape(2 * X, X)
    wide_second = twin(spread)
    place = (jnp.arange(XW, dtype=jnp.int32) % PAIR) // 2
    keep = (place >= LOCAL).astype(F32)[:, None]
    wide_vert = stack_terms(wide_first, wide_second, keep, jnp.repeat(modes, 2))

    vmem = pl.BlockSpec(memory_space=pltpu.VMEM)
    smem = pl.BlockSpec(memory_space=pltpu.SMEM)
    hbm = pl.BlockSpec(memory_space=pltpu.HBM)
    peers = count * LEV
    rowed = (FL, RQ * R5, 2, waves)
    block = jax.ShapeDtypeStruct((peers, ROWS, LANES), BF16)
    block_scratch = pltpu.VMEM((LANES // 128, peers * ROWS, 128), F32)

    sent = pl.pallas_call(
        select_kernel,
        in_specs=[vmem, hbm],
        out_specs=hbm,
        out_shape=block,
        scratch_shapes=[
            pltpu.VMEM(rowed, BF16),
            pltpu.VMEM((RQ, SIDE, waves), BF16),
            block_scratch,
            pltpu.VMEM(block.shape, BF16),
            pltpu.SemaphoreType.DMA((RQ,)),
            pltpu.SemaphoreType.DMA((CUTS,)),
        ],
        compiler_params=params(60),
        name="select_waves",
    )(wave_order, fourier.transpose(0, 2, 3, 1, 4).reshape(rowed))
    arrived = lax.all_to_all(sent, ("lev", "wave"), split_axis=0, concat_axis=0, tiled=True)
    solved = pl.pallas_call(
        spectral_kernel,
        in_specs=[smem] + [vmem] * 4 + [hbm],
        out_specs=vmem,
        out_shape=block,
        scratch_shapes=[
            pltpu.VMEM((lat_count, lat_count), BF16),
            block_scratch,
            pltpu.VMEM((TOTAL, lat_count), BF16),
            pltpu.VMEM((TOTAL, lat_half), BF16),
            pltpu.VMEM((TOTAL, lat_half), BF16),
            pltpu.VMEM((LEV, WIDE, RQ * count), F32),
            pltpu.VMEM((3,) + legendre.shape[1:], BF16),
            pltpu.SemaphoreType.DMA((3,)),
        ],
        compiler_params=params(46),
        name="spectral_round",
    )(places, arrived, rows_in, vert, wide_vert, legendre)
    returned = lax.all_to_all(solved, ("lev", "wave"), split_axis=0, concat_axis=0, tiled=True)
    restored = pl.pallas_call(
        restore_kernel,
        in_specs=[vmem] * 2,
        out_specs=hbm,
        out_shape=jax.ShapeDtypeStruct(rowed, BF16),
        scratch_shapes=[
            block_scratch,
            pltpu.VMEM(rowed, BF16),
            pltpu.SemaphoreType.DMA((RQ,)),
        ],
        compiler_params=params(48),
        name="restore_waves",
    )(wave_order, returned)
    restored = restored.reshape(2, LOCAL, RQ * R5, 2, waves)
    return restored.transpose(0, 3, 1, 2, 4)


def solution(mesh):
    placed = (
        P(None, None, "lev", "wave", None),
        P(),
        P(),
        P(),
        P("wave", None, None),
        P(),
        P(),
        P(),
        P(),
        P(),
        P(),
    )
    return jax.shard_map(
        local,
        mesh=mesh,
        in_specs=placed,
        out_specs=P(None, None, "lev", "wave", None),
        check_vma=False,
    )
```

```python
import jax
import jax.numpy as jnp
from jax import lax
from jax.experimental import pallas as pl
from jax.experimental.pallas import tpu as pltpu
from jax.sharding import PartitionSpec as P

RQ, R5 = 4, 5
ROWS = 8
LANES = 512
LEV = 4
LOCAL = 18
X = LEV * LOCAL
FL = 2 * LOCAL
UNIT = 40
XP = LEV * UNIT
PAIR = 2 * FL
XW = LEV * PAIR
SIDE = 384
HALF = 2 * SIDE
WIDE = 2 * LANES
TOTAL = 2 * XW + XP
WHOLE = ((0, 1), (3, 4), (5, 6), (8, 9))
SHARED = (2, 7)
CUTS = 4
NT = (((1,), (1,)), ((), ()))
TN = (((0,), (0,)), ((), ()))
NN = (((1,), (0,)), ((), ()))
F32 = jnp.float32
BF16 = jnp.bfloat16


def dot(a, b, dims):
    return lax.dot_general(a, b, dims, preferred_element_type=F32)


def params(mebibytes):
    return pltpu.CompilerParams(vmem_limit_bytes=mebibytes * 1024 * 1024)


def put_rows(scr, start, size, stride, values):
    width = scr.shape[2]
    for t in range(scr.shape[0]):
        scr[t, pl.ds(start, size, stride=stride), :] = values[:, t * width : (t + 1) * width]


def get_rows(scr, start, size, stride):
    tiles = [scr[t, pl.ds(start, size, stride=stride), :] for t in range(scr.shape[0])]
    return jnp.concatenate(tiles, axis=1)


def put_block(scr, block_ref):
    width = scr.shape[2]
    for t in range(scr.shape[0]):
        part = block_ref[:, :, t * width : (t + 1) * width].astype(F32)
        scr[t] = part.reshape(scr.shape[1:])


def get_block(scr, out_ref, first, last):
    width = scr.shape[2]
    for t in range(scr.shape[0]):
        part = scr[t, first * ROWS : last * ROWS, :].reshape(last - first, ROWS, width)
        out_ref[first:last, :, t * width : (t + 1) * width] = part.astype(BF16)


def send_block(scr, out_buf, out_hbm, out_sem):
    step = out_buf.shape[0] // CUTS
    stores = []
    for cut in range(CUTS):
        get_block(scr, out_buf, cut * step, (cut + 1) * step)
        part = pl.ds(cut * step, step)
        stores.append(pltpu.make_async_copy(out_buf.at[part], out_hbm.at[part], out_sem.at[cut]))
        stores[-1].start()
    for store in stores:
        store.wait()


def h_block(lat_half):
    return 128 if lat_half % 128 == 0 else lat_half


def wave_matrix(wave_ref, peers):
    count = wave_ref.shape[0]
    m_local = count // peers
    row = lax.broadcasted_iota(jnp.int32, (count, 1), 0)
    ids = lax.broadcasted_iota(jnp.int32, (count, count), 1)
    slot = lax.rem(row, peers) * m_local + lax.div(row, peers)
    waves = wave_ref[...].reshape(1, count).astype(F32)
    held = jnp.sum(jnp.where(ids == slot, waves, 0.0), axis=1, keepdims=True)
    return jnp.where(held == ids.astype(F32), 1.0, 0.0).astype(BF16)


def fill_lat_matrix(rows_ref, ot_scr):
    lat_count = ot_scr.shape[0]
    half = lat_count // 2
    hb = h_block(half)
    at = rows_ref.shape[0] - 3
    lats = jnp.concatenate([rows_ref[at : at + 1, :], rows_ref[at + 1 : at + 2, :]], axis=1)
    lats = lats.astype(jnp.int32)
    for block in range(half // hb):
        ids = lax.broadcasted_iota(jnp.int32, (hb, lat_count), 0) + block * hb
        north = jnp.where(lats == ids, 1.0, 0.0).astype(BF16)
        south = jnp.where(lats == lat_count - 1 - ids, 1.0, 0.0).astype(BF16)
        ot_scr[2 * block * hb : (2 * block + 1) * hb, :] = north
        ot_scr[(2 * block + 1) * hb : (2 * block + 2) * hb, :] = south


def part_matrix():
    row = lax.broadcasted_iota(jnp.int32, (SIDE, 2 * (WIDE - HALF)), 0)
    lane = lax.broadcasted_iota(jnp.int32, (1, 2 * (WIDE - HALF)), 1)
    c = lax.div(lane, WIDE - HALF)
    inner = lax.rem(lane, WIDE - HALF)
    unit, fl = lax.div(inner, UNIT), lax.rem(inner, UNIT)
    source = jnp.where((unit < R5) & (fl < FL), unit * PAIR + fl * 2 + c, -1)
    return jnp.where(row == source, 1.0, 0.0).astype(BF16)


def select_kernel(wave_ref, x_hbm, out_hbm, x_buf, z_scr, scr, out_buf, in_sem, out_sem):
    waves = z_scr.shape[2]
    peers = out_buf.shape[0] // LEV
    loads = []
    for rq in range(RQ):
        part = pl.ds(rq * R5, R5)
        loads.append(pltpu.make_async_copy(x_hbm.at[:, part], x_buf.at[:, part], in_sem.at[rq]))
        loads[-1].start()
    onehot = wave_matrix(wave_ref, peers)
    apart = part_matrix()
    z_scr[:, R5 * PAIR :, :] = jnp.zeros((RQ, SIDE - R5 * PAIR, waves), BF16)
    for rq in range(RQ):
        loads[rq].wait()
        for r5 in range(R5):
            piece = x_buf[:, rq * R5 + r5].reshape(PAIR, waves)
            z_scr[rq, r5 * PAIR : (r5 + 1) * PAIR, :] = piece
    for rq in range(RQ):
        got = dot(onehot, z_scr[rq], NT)

        def put(peer, tile, values):
            for t in range(values.shape[1] // 128):
                side, lane = (tile + t) // 4, (tile + t) % 4
                start = peer * peers * ROWS + rq * 2 + side
                scr[lane, pl.ds(start, peers, stride=ROWS), :] = values[:, t * 128 : (t + 1) * 128]

        for peer in range(LEV):
            for i, kk in enumerate(WHOLE[peer]):
                put(peer, 3 * i, got[kk * peers : (kk + 1) * peers])
        both = jnp.concatenate([got[kk * peers : (kk + 1) * peers] for kk in SHARED], axis=0)
        both = dot(both.astype(BF16), apart, NN)
        for peer in range(LEV):
            rows = both[(peer // 2) * peers : (peer // 2 + 1) * peers]
            put(peer, 6, rows[:, (peer % 2) * (WIDE - HALF) : (peer % 2 + 1) * (WIDE - HALF)])
    send_block(scr, out_buf, out_hbm, out_sem)


def slots_of(p):
    for i in range(2):
        yield i * SIDE, PAIR, i * XW + p * PAIR
    yield HALF, UNIT, 2 * XW + p * UNIT


def solve(state_low, factor, first, second, keep, modes):
    size = modes.shape[0]
    mixed = dot(first, jnp.concatenate([state_low, state_low], axis=0), NN)
    modal = (mixed[:size] + factor * mixed[size:]) / (1.0 + factor * modes)
    high = modal.astype(BF16).astype(F32)
    stacked = jnp.concatenate([high, modal - high, high], axis=0).astype(BF16)
    new = dot(second, stacked, NN)
    return (new + keep * state_low.astype(F32)).astype(BF16)


def spectral_kernel(
    place_ref, r_ref, rows_ref, vert_hbm, wide_hbm, leg_hbm, out_ref,
    ot_scr, scr, lat_scr, sym_scr, anti_scr, band_scr, leg_buf, leg_sem, vert_ref, wide_ref, solve_sem,
):
    peers = r_ref.shape[0] // LEV
    half = ot_scr.shape[0] // 2
    hb = h_block(half)
    span = 2 * peers
    waves = rows_ref.shape[1]
    me = place_ref[place_ref.shape[0] - 1]
    whole = lax.div(5 * me + 1, 2)
    held = (whole, whole + 1, 2 + 5 * lax.div(me, 2))
    loads = []
    for i, kk in enumerate(held):
        loads.append(pltpu.make_async_copy(leg_hbm.at[kk], leg_buf.at[i], leg_sem.at[i]))
        loads[-1].start()
    solve_loads = [
        pltpu.make_async_copy(vert_hbm, vert_ref, solve_sem.at[0]),
        pltpu.make_async_copy(wide_hbm, wide_ref, solve_sem.at[1]),
    ]
    for load in solve_loads:
        load.start()
    fill_lat_matrix(rows_ref, ot_scr)
    put_block(scr, r_ref)
    for p in range(LEV):
        for pair in range(RQ // 2):
            part = jnp.concatenate(
                [
                    jnp.concatenate(
                        [get_rows(scr, p * peers * ROWS + 2 * rq + side, peers, ROWS) for side in range(2)],
                        axis=1,
                    )
                    for rq in (2 * pair, 2 * pair + 1)
                ],
                axis=0,
            )
            turned = part.T
            for at, size, row in slots_of(p):
                for r5 in range(R5):
                    lane = (r5 * 2 + pair) * span
                    piece = turned[at + r5 * size : at + (r5 + 1) * size]
                    lat_scr[row : row + size, lane : lane + span] = piece.astype(BF16)
    lhs = lat_scr[...]
    for block in range(half // hb):
        both = dot(lhs, ot_scr[2 * block * hb : (2 * block + 2) * hb, :], NT)
        north, south = both[:, :hb], both[:, hb:]
        weight = rows_ref[rows_ref.shape[0] - 1 :, block * hb : (block + 1) * hb]
        sym_scr[:, block * hb : (block + 1) * hb] = ((north + south) * weight).astype(BF16)
        anti_scr[:, block * hb : (block + 1) * hb] = ((north - south) * weight).astype(BF16)

    for load in solve_loads:
        load.wait()
    wide, narrow = (
        (
            ref[: 2 * size, : 2 * span_in].astype(BF16),
            ref[2 * size :, : 3 * size].astype(BF16),
            ref[2 * size :, 3 * size : 3 * size + 1],
            ref[2 * size : 3 * size, 3 * size + 1 : 3 * size + 2],
        )
        for ref, size, span_in in ((wide_ref, 2 * X, XW), (vert_ref, X, XP))
    )
    degree = lax.broadcasted_iota(jnp.int32, (1, waves), 1)
    factor = (degree * (degree + 1)).astype(F32) / float(waves * (waves + 1))
    for i, kk in enumerate(held):
        low, size = i * XW, XW if i < 2 else XP
        live = rows_ref[pl.ds(kk, 1), :]
        even = lax.rem(degree + place_ref[kk], 2) == 0
        loads[i].wait()
        leg = leg_buf[i]
        sym = dot(sym_scr[low : low + size, :], leg, NT)
        anti = dot(anti_scr[low : low + size, :], leg, NT)
        state_low = (jnp.where(even, sym, anti) * live).astype(BF16)
        new = solve(state_low, factor, *(wide if i < 2 else narrow)).astype(F32) * live
        signed = jnp.where(even, new, -new)
        north = dot(new.astype(BF16), leg, NN).astype(BF16)
        south = dot(signed.astype(BF16), leg, NN).astype(BF16)
        for block in range(half // hb):
            lane = 2 * block * hb
            lat_scr[low : low + size, lane : lane + hb] = north[:, block * hb : (block + 1) * hb]
            lat_scr[low : low + size, lane + hb : lane + 2 * hb] = south[:, block * hb : (block + 1) * hb]

    lhs = lat_scr[...]
    for r5 in range(R5):
        band = dot(lhs, ot_scr[:, 2 * r5 * span : 2 * (r5 + 1) * span], NN)
        for p in range(LEV):
            for at, size, row in slots_of(p):
                band_scr[p, at + r5 * size : at + (r5 + 1) * size, :] = band[row : row + size]
    for p in range(LEV):
        for pair in range(RQ // 2):
            turned = band_scr[p, :, pair * span : (pair + 1) * span].T
            for i in range(2):
                for side in range(2):
                    start = p * peers * ROWS + (2 * pair + i) * 2 + side
                    piece = turned[i * peers : (i + 1) * peers, side * LANES : (side + 1) * LANES]
                    put_rows(scr, start, peers, ROWS, piece)
    get_block(scr, out_ref, 0, out_ref.shape[0])


def restore_kernel(wave_ref, r_ref, out_hbm, scr, out_buf, out_sem):
    peers = r_ref.shape[0] // LEV
    waves = wave_ref.shape[0]
    onehot = wave_matrix(wave_ref, peers)
    apart = part_matrix()
    put_block(scr, r_ref)
    stores = []
    for rq in range(RQ):

        def get(peer, tile, tiles):
            values = []
            for t in range(tile, tile + tiles):
                start = peer * peers * ROWS + rq * 2 + t // 4
                values.append(scr[t % 4, pl.ds(start, peers, stride=ROWS), :])
            return jnp.concatenate(values, axis=1)

        parts = {}
        for peer in range(LEV):
            for i, kk in enumerate(WHOLE[peer]):
                parts[kk] = get(peer, 3 * i, 3)
        lane = lax.broadcasted_iota(jnp.int32, (peers, WIDE - HALF), 1)
        shared = [
            jnp.concatenate(
                [jnp.where(lane < R5 * UNIT, get(2 * i + c, 6, 2), 0.0) for c in range(2)], axis=1
            )
            for i in range(2)
        ]
        shared = dot(jnp.concatenate(shared, axis=0).astype(BF16), apart, NT)
        for i, kk in enumerate(SHARED):
            parts[kk] = shared[i * peers : (i + 1) * peers]
        part = jnp.concatenate([parts[kk] for kk in sorted(parts)], axis=0).astype(BF16)
        got = dot(part, onehot, TN).astype(BF16)
        for r5 in range(R5):
            piece = got[r5 * PAIR : (r5 + 1) * PAIR].reshape(FL, 2, waves)
            out_buf[:, rq * R5 + r5] = piece
        part = pl.ds(rq * R5, R5)
        stores.append(pltpu.make_async_copy(out_buf.at[:, part], out_hbm.at[:, part], out_sem.at[rq]))
        stores[-1].start()
    for store in stores:
        store.wait()


def stack_terms(first, second, keep, modes):
    def parts(matrix):
        high = lax.reduce_precision(matrix, 8, 7)
        return high, matrix - high

    first_high, first_low = parts(first)
    second_high, second_low = parts(second)
    rows, size = second.shape
    column = jnp.pad(modes, (0, rows - size))[:, None]
    top = jnp.concatenate([first_high, first_low], axis=1)
    bottom = jnp.concatenate([second_high, second_high, second_low, keep, column], axis=1)
    bottom = jnp.pad(bottom, ((0, 0), (0, top.shape[1] - bottom.shape[1])))
    return jnp.concatenate([top, bottom], axis=0)


def local(
    fourier,
    lat_order,
    wave_order,
    pattern,
    legendre,
    lat_weight,
    hydrostatic_thermal_link,
    evec,
    einv,
    spread_to_heat_link,
    modes,
):
    m_local, waves, lat_half = legendre.shape
    lat_count = 2 * lat_half
    count = waves // m_local
    block_count = pattern.shape[0]
    block_width = waves // block_count
    high = lax.Precision.HIGHEST

    lat_rows = lat_order.reshape(count, RQ, R5).transpose(2, 1, 0).reshape(2, lat_half).astype(F32)
    my_waves = lax.dynamic_slice_in_dim(wave_order, lax.axis_index("wave") * m_local, m_local)
    owner_rows = (
        my_waves[:, None] // block_width == jnp.arange(block_count, dtype=jnp.int32)[None, :]
    ).astype(F32)
    live_rows = jnp.dot(owner_rows, pattern.astype(F32), precision=high)
    live = jnp.repeat(live_rows, block_width, axis=1)
    rows_in = jnp.concatenate([live, lat_rows, lat_weight[None, :]], axis=0)
    places = jnp.concatenate([my_waves, lax.axis_index("lev")[None]]).astype(jnp.int32)

    einv_link = jnp.dot(einv, hydrostatic_thermal_link, precision=high)
    heat_evec = jnp.dot(spread_to_heat_link, evec, precision=high)
    gap = ((0, 0), (0, UNIT - FL), (0, 0))
    none = jnp.zeros((X, LEV, LOCAL), F32)
    tail = jnp.zeros((X, LEV, UNIT - FL), F32)
    first = jnp.concatenate(
        [
            jnp.concatenate([einv.reshape(X, LEV, LOCAL), none, tail], axis=2),
            jnp.concatenate([none, einv_link.reshape(X, LEV, LOCAL), tail], axis=2),
        ],
        axis=0,
    ).reshape(2 * X, XP)
    second = jnp.concatenate(
        [evec.reshape(LEV, LOCAL, X), -heat_evec.reshape(LEV, LOCAL, X)], axis=1
    )
    second = jnp.pad(second, gap).reshape(XP, X)
    place = jnp.arange(XP, dtype=jnp.int32) % UNIT
    keep = ((place >= LOCAL) & (place < FL)).astype(F32)[:, None]
    vert = stack_terms(first, second, keep, modes)

    def twin(matrix):
        rows, columns = matrix.shape
        down = jnp.arange(2 * rows, dtype=jnp.int32)[:, None]
        across = jnp.arange(2 * columns, dtype=jnp.int32)[None, :]
        left = (down // 2 == jnp.arange(rows, dtype=jnp.int32)[None, :]).astype(F32)
        right = (across // 2 == jnp.arange(columns, dtype=jnp.int32)[:, None]).astype(F32)
        spread = jnp.dot(jnp.dot(left, matrix, precision=high), right, precision=high)
        return jnp.where(down % 2 == across % 2, spread, 0.0)

    none = jnp.zeros((X, LEV, LOCAL), F32)
    fold = jnp.stack(
        [
            jnp.concatenate([einv.reshape(X, LEV, LOCAL), none], axis=2),
            jnp.concatenate([none, einv_link.reshape(X, LEV, LOCAL)], axis=2),
        ]
    ).reshape(2 * X, 2 * X)
    wide_first = twin(fold)
    spread = jnp.concatenate(
        [evec.reshape(LEV, LOCAL, X), -heat_evec.reshape(LEV, LOCAL, X)], axis=1
    ).reshape(2 * X, X)
    wide_second = twin(spread)
    place = (jnp.arange(XW, dtype=jnp.int32) % PAIR) // 2
    keep = (place >= LOCAL).astype(F32)[:, None]
    wide_vert = stack_terms(wide_first, wide_second, keep, jnp.repeat(modes, 2))

    vmem = pl.BlockSpec(memory_space=pltpu.VMEM)
    smem = pl.BlockSpec(memory_space=pltpu.SMEM)
    hbm = pl.BlockSpec(memory_space=pltpu.HBM)
    peers = count * LEV
    rowed = (FL, RQ * R5, 2, waves)
    block = jax.ShapeDtypeStruct((peers, ROWS, LANES), BF16)
    block_scratch = pltpu.VMEM((LANES // 128, peers * ROWS, 128), F32)

    sent = pl.pallas_call(
        select_kernel,
        in_specs=[vmem, hbm],
        out_specs=hbm,
        out_shape=block,
        scratch_shapes=[
            pltpu.VMEM(rowed, BF16),
            pltpu.VMEM((RQ, SIDE, waves), BF16),
            block_scratch,
            pltpu.VMEM(block.shape, BF16),
            pltpu.SemaphoreType.DMA((RQ,)),
            pltpu.SemaphoreType.DMA((CUTS,)),
        ],
        compiler_params=params(60),
        name="select_waves",
    )(wave_order, fourier.transpose(0, 2, 3, 1, 4).reshape(rowed))
    arrived = lax.all_to_all(sent, ("lev", "wave"), split_axis=0, concat_axis=0, tiled=True)
    solved = pl.pallas_call(
        spectral_kernel,
        in_specs=[smem] + [vmem] * 2 + [hbm] * 3,
        out_specs=vmem,
        out_shape=block,
        scratch_shapes=[
            pltpu.VMEM((lat_count, lat_count), BF16),
            block_scratch,
            pltpu.VMEM((TOTAL, lat_count), BF16),
            pltpu.VMEM((TOTAL, lat_half), BF16),
            pltpu.VMEM((TOTAL, lat_half), BF16),
            pltpu.VMEM((LEV, WIDE, RQ * count), F32),
            pltpu.VMEM((3,) + legendre.shape[1:], BF16),
            pltpu.SemaphoreType.DMA((3,)),
            pltpu.VMEM(vert.shape, F32),
            pltpu.VMEM(wide_vert.shape, F32),
            pltpu.SemaphoreType.DMA((2,)),
        ],
        compiler_params=params(46),
        name="spectral_round",
    )(places, arrived, rows_in, vert, wide_vert, legendre)
    returned = lax.all_to_all(solved, ("lev", "wave"), split_axis=0, concat_axis=0, tiled=True)
    restored = pl.pallas_call(
        restore_kernel,
        in_specs=[vmem] * 2,
        out_specs=hbm,
        out_shape=jax.ShapeDtypeStruct(rowed, BF16),
        scratch_shapes=[
            block_scratch,
            pltpu.VMEM(rowed, BF16),
            pltpu.SemaphoreType.DMA((RQ,)),
        ],
        compiler_params=params(48),
        name="restore_waves",
    )(wave_order, returned)
    restored = restored.reshape(2, LOCAL, RQ * R5, 2, waves)
    return restored.transpose(0, 3, 1, 2, 4)


def solution(mesh):
    placed = (
        P(None, None, "lev", "wave", None),
        P(),
        P(),
        P(),
        P("wave", None, None),
        P(),
        P(),
        P(),
        P(),
        P(),
        P(),
    )
    return jax.shard_map(
        local,
        mesh=mesh,
        in_specs=placed,
        out_specs=P(None, None, "lev", "wave", None),
        check_vma=False,
    )
```

```python
import jax
import jax.numpy as jnp
from jax import lax
from jax.experimental import pallas as pl
from jax.experimental.pallas import tpu as pltpu
from jax.sharding import PartitionSpec as P

RQ, R5 = 4, 5
ROWS = 8
LANES = 512
LEV = 4
LOCAL = 18
X = LEV * LOCAL
FL = 2 * LOCAL
UNIT = 40
XP = LEV * UNIT
PAIR = 2 * FL
XW = LEV * PAIR
SIDE = 384
HALF = 2 * SIDE
WIDE = 2 * LANES
TOTAL = 2 * XW + XP
WHOLE = ((0, 1), (3, 4), (5, 6), (8, 9))
SHARED = (2, 7)
CUTS = 4
NT = (((1,), (1,)), ((), ()))
TN = (((0,), (0,)), ((), ()))
NN = (((1,), (0,)), ((), ()))
F32 = jnp.float32
BF16 = jnp.bfloat16


def dot(a, b, dims):
    return lax.dot_general(a, b, dims, preferred_element_type=F32)


def params(mebibytes):
    return pltpu.CompilerParams(vmem_limit_bytes=mebibytes * 1024 * 1024)


def put_rows(scr, start, size, stride, values):
    width = scr.shape[2]
    for t in range(scr.shape[0]):
        scr[t, pl.ds(start, size, stride=stride), :] = values[:, t * width : (t + 1) * width]


def get_rows(scr, start, size, stride):
    tiles = [scr[t, pl.ds(start, size, stride=stride), :] for t in range(scr.shape[0])]
    return jnp.concatenate(tiles, axis=1)


def put_block(scr, block_ref):
    width = scr.shape[2]
    for t in range(scr.shape[0]):
        part = block_ref[:, :, t * width : (t + 1) * width].astype(F32)
        scr[t] = part.reshape(scr.shape[1:])


def get_block(scr, out_ref, first, last):
    width = scr.shape[2]
    for t in range(scr.shape[0]):
        part = scr[t, first * ROWS : last * ROWS, :].reshape(last - first, ROWS, width)
        out_ref[first:last, :, t * width : (t + 1) * width] = part.astype(BF16)


def send_block(scr, out_buf, out_hbm, out_sem):
    step = out_buf.shape[0] // CUTS
    stores = []
    for cut in range(CUTS):
        get_block(scr, out_buf, cut * step, (cut + 1) * step)
        part = pl.ds(cut * step, step)
        stores.append(pltpu.make_async_copy(out_buf.at[part], out_hbm.at[part], out_sem.at[cut]))
        stores[-1].start()
    for store in stores:
        store.wait()


def h_block(lat_half):
    return 128 if lat_half % 128 == 0 else lat_half


def wave_matrix(wave_ref, peers):
    count = wave_ref.shape[0]
    m_local = count // peers
    row = lax.broadcasted_iota(jnp.int32, (count, 1), 0)
    ids = lax.broadcasted_iota(jnp.int32, (count, count), 1)
    slot = lax.rem(row, peers) * m_local + lax.div(row, peers)
    waves = wave_ref[...].reshape(1, count).astype(F32)
    held = jnp.sum(jnp.where(ids == slot, waves, 0.0), axis=1, keepdims=True)
    return jnp.where(held == ids.astype(F32), 1.0, 0.0).astype(BF16)


def fill_lat_matrix(rows_ref, ot_scr):
    lat_count = ot_scr.shape[0]
    half = lat_count // 2
    hb = h_block(half)
    at = rows_ref.shape[0] - 3
    lats = jnp.concatenate([rows_ref[at : at + 1, :], rows_ref[at + 1 : at + 2, :]], axis=1)
    lats = lats.astype(jnp.int32)
    for block in range(half // hb):
        ids = lax.broadcasted_iota(jnp.int32, (hb, lat_count), 0) + block * hb
        north = jnp.where(lats == ids, 1.0, 0.0).astype(BF16)
        south = jnp.where(lats == lat_count - 1 - ids, 1.0, 0.0).astype(BF16)
        ot_scr[2 * block * hb : (2 * block + 1) * hb, :] = north
        ot_scr[(2 * block + 1) * hb : (2 * block + 2) * hb, :] = south


def part_matrix():
    row = lax.broadcasted_iota(jnp.int32, (SIDE, 2 * (WIDE - HALF)), 0)
    lane = lax.broadcasted_iota(jnp.int32, (1, 2 * (WIDE - HALF)), 1)
    c = lax.div(lane, WIDE - HALF)
    inner = lax.rem(lane, WIDE - HALF)
    unit, fl = lax.div(inner, UNIT), lax.rem(inner, UNIT)
    source = jnp.where((unit < R5) & (fl < FL), unit * PAIR + fl * 2 + c, -1)
    return jnp.where(row == source, 1.0, 0.0).astype(BF16)


def select_kernel(wave_ref, x_hbm, out_hbm, x_buf, z_scr, scr, out_buf, in_sem, out_sem):
    waves = z_scr.shape[2]
    peers = out_buf.shape[0] // LEV
    loads = []
    for rq in range(RQ):
        part = pl.ds(rq * R5, R5)
        loads.append(pltpu.make_async_copy(x_hbm.at[:, part], x_buf.at[:, part], in_sem.at[rq]))
        loads[-1].start()
    onehot = wave_matrix(wave_ref, peers)
    apart = part_matrix()
    z_scr[:, R5 * PAIR :, :] = jnp.zeros((RQ, SIDE - R5 * PAIR, waves), BF16)
    for rq in range(RQ):
        loads[rq].wait()
        for r5 in range(R5):
            piece = x_buf[:, rq * R5 + r5].reshape(PAIR, waves)
            z_scr[rq, r5 * PAIR : (r5 + 1) * PAIR, :] = piece
    for rq in range(RQ):
        got = dot(onehot, z_scr[rq], NT)

        def put(peer, tile, values):
            for t in range(values.shape[1] // 128):
                side, lane = (tile + t) // 4, (tile + t) % 4
                start = peer * peers * ROWS + rq * 2 + side
                scr[lane, pl.ds(start, peers, stride=ROWS), :] = values[:, t * 128 : (t + 1) * 128]

        for peer in range(LEV):
            for i, kk in enumerate(WHOLE[peer]):
                put(peer, 3 * i, got[kk * peers : (kk + 1) * peers])
        both = jnp.concatenate([got[kk * peers : (kk + 1) * peers] for kk in SHARED], axis=0)
        both = dot(both.astype(BF16), apart, NN)
        for peer in range(LEV):
            rows = both[(peer // 2) * peers : (peer // 2 + 1) * peers]
            put(peer, 6, rows[:, (peer % 2) * (WIDE - HALF) : (peer % 2 + 1) * (WIDE - HALF)])
    send_block(scr, out_buf, out_hbm, out_sem)


def slots_of(p):
    for i in range(2):
        yield i * SIDE, PAIR, i * XW + p * PAIR
    yield HALF, UNIT, 2 * XW + p * UNIT


def split(values):
    high = values.astype(BF16)
    return high, (values - high.astype(F32)).astype(BF16)


def solve(state_low, factor, first, second, keep, modes):
    first_high, first_low = first
    second_high, second_low = second
    size = modes.shape[0]
    mixed = dot(first_high, state_low, NN) + dot(first_low, state_low, NN)
    modal = (mixed[:size] + factor * mixed[size:]) / (1.0 + factor * modes)
    modal_high, modal_low = split(modal)
    new = (
        dot(second_high, modal_high, NN)
        + dot(second_high, modal_low, NN)
        + dot(second_low, modal_high, NN)
    )
    return (new + keep * state_low.astype(F32)).astype(BF16)


def spectral_kernel(
    place_ref, r_ref, rows_ref, vert_ref, wide_ref, leg_hbm, out_ref,
    ot_scr, scr, lat_scr, sym_scr, anti_scr, band_scr, leg_buf, leg_sem,
):
    peers = r_ref.shape[0] // LEV
    half = ot_scr.shape[0] // 2
    hb = h_block(half)
    span = 2 * peers
    waves = rows_ref.shape[1]
    me = place_ref[place_ref.shape[0] - 1]
    whole = lax.div(5 * me + 1, 2)
    held = (whole, whole + 1, 2 + 5 * lax.div(me, 2))
    loads = []
    for i, kk in enumerate(held):
        loads.append(pltpu.make_async_copy(leg_hbm.at[kk], leg_buf.at[i], leg_sem.at[i]))
        loads[-1].start()
    fill_lat_matrix(rows_ref, ot_scr)
    put_block(scr, r_ref)
    for p in range(LEV):
        for pair in range(RQ // 2):
            part = jnp.concatenate(
                [
                    jnp.concatenate(
                        [get_rows(scr, p * peers * ROWS + 2 * rq + side, peers, ROWS) for side in range(2)],
                        axis=1,
                    )
                    for rq in (2 * pair, 2 * pair + 1)
                ],
                axis=0,
            )
            turned = part.T
            for at, size, row in slots_of(p):
                for r5 in range(R5):
                    lane = (r5 * 2 + pair) * span
                    piece = turned[at + r5 * size : at + (r5 + 1) * size]
                    lat_scr[row : row + size, lane : lane + span] = piece.astype(BF16)
    lhs = lat_scr[...]
    for block in range(half // hb):
        both = dot(lhs, ot_scr[2 * block * hb : (2 * block + 2) * hb, :], NT)
        north, south = both[:, :hb], both[:, hb:]
        weight = rows_ref[rows_ref.shape[0] - 1 :, block * hb : (block + 1) * hb]
        sym_scr[:, block * hb : (block + 1) * hb] = ((north + south) * weight).astype(BF16)
        anti_scr[:, block * hb : (block + 1) * hb] = ((north - south) * weight).astype(BF16)

    wide, narrow = (
        (
            split(ref[: 2 * size, :span_in]),
            split(ref[2 * size :, :size]),
            ref[2 * size :, size : size + 1],
            ref[2 * size : 3 * size, size + 1 : size + 2],
        )
        for ref, size, span_in in ((wide_ref, 2 * X, XW), (vert_ref, X, XP))
    )
    degree = lax.broadcasted_iota(jnp.int32, (1, waves), 1)
    factor = (degree * (degree + 1)).astype(F32) / float(waves * (waves + 1))
    for i, kk in enumerate(held):
        low, size = i * XW, XW if i < 2 else XP
        live = rows_ref[pl.ds(kk, 1), :]
        even = lax.rem(degree + place_ref[kk], 2) == 0
        loads[i].wait()
        leg = leg_buf[i]
        sym = dot(sym_scr[low : low + size, :], leg, NT)
        anti = dot(anti_scr[low : low + size, :], leg, NT)
        state_low = (jnp.where(even, sym, anti) * live).astype(BF16)
        new = solve(state_low, factor, *(wide if i < 2 else narrow)).astype(F32) * live
        signed = jnp.where(even, new, -new)
        north = dot(new.astype(BF16), leg, NN).astype(BF16)
        south = dot(signed.astype(BF16), leg, NN).astype(BF16)
        for block in range(half // hb):
            lane = 2 * block * hb
            lat_scr[low : low + size, lane : lane + hb] = north[:, block * hb : (block + 1) * hb]
            lat_scr[low : low + size, lane + hb : lane + 2 * hb] = south[:, block * hb : (block + 1) * hb]

    lhs = lat_scr[...]
    for r5 in range(R5):
        band = dot(lhs, ot_scr[:, 2 * r5 * span : 2 * (r5 + 1) * span], NN)
        for p in range(LEV):
            for at, size, row in slots_of(p):
                band_scr[p, at + r5 * size : at + (r5 + 1) * size, :] = band[row : row + size]
    for p in range(LEV):
        for pair in range(RQ // 2):
            turned = band_scr[p, :, pair * span : (pair + 1) * span].T
            for i in range(2):
                for side in range(2):
                    start = p * peers * ROWS + (2 * pair + i) * 2 + side
                    piece = turned[i * peers : (i + 1) * peers, side * LANES : (side + 1) * LANES]
                    put_rows(scr, start, peers, ROWS, piece)
    get_block(scr, out_ref, 0, out_ref.shape[0])


def restore_kernel(wave_ref, r_ref, out_hbm, scr, out_buf, out_sem):
    peers = r_ref.shape[0] // LEV
    waves = wave_ref.shape[0]
    onehot = wave_matrix(wave_ref, peers)
    apart = part_matrix()
    put_block(scr, r_ref)
    stores = []
    for rq in range(RQ):

        def get(peer, tile, tiles):
            values = []
            for t in range(tile, tile + tiles):
                start = peer * peers * ROWS + rq * 2 + t // 4
                values.append(scr[t % 4, pl.ds(start, peers, stride=ROWS), :])
            return jnp.concatenate(values, axis=1)

        parts = {}
        for peer in range(LEV):
            for i, kk in enumerate(WHOLE[peer]):
                parts[kk] = get(peer, 3 * i, 3)
        lane = lax.broadcasted_iota(jnp.int32, (peers, WIDE - HALF), 1)
        shared = [
            jnp.concatenate(
                [jnp.where(lane < R5 * UNIT, get(2 * i + c, 6, 2), 0.0) for c in range(2)], axis=1
            )
            for i in range(2)
        ]
        shared = dot(jnp.concatenate(shared, axis=0).astype(BF16), apart, NT)
        for i, kk in enumerate(SHARED):
            parts[kk] = shared[i * peers : (i + 1) * peers]
        part = jnp.concatenate([parts[kk] for kk in sorted(parts)], axis=0).astype(BF16)
        got = dot(part, onehot, TN).astype(BF16)
        for r5 in range(R5):
            piece = got[r5 * PAIR : (r5 + 1) * PAIR].reshape(FL, 2, waves)
            out_buf[:, rq * R5 + r5] = piece
        part = pl.ds(rq * R5, R5)
        stores.append(pltpu.make_async_copy(out_buf.at[:, part], out_hbm.at[:, part], out_sem.at[rq]))
        stores[-1].start()
    for store in stores:
        store.wait()


def stack_terms(first, second, keep, modes):
    rows, size = second.shape
    column = jnp.pad(modes, (0, rows - size))[:, None]
    bottom = jnp.concatenate([second, keep, column], axis=1)
    bottom = jnp.pad(bottom, ((0, 0), (0, first.shape[1] - bottom.shape[1])))
    return jnp.concatenate([first, bottom], axis=0)


def local(
    fourier,
    lat_order,
    wave_order,
    pattern,
    legendre,
    lat_weight,
    hydrostatic_thermal_link,
    evec,
    einv,
    spread_to_heat_link,
    modes,
):
    m_local, waves, lat_half = legendre.shape
    lat_count = 2 * lat_half
    count = waves // m_local
    block_count = pattern.shape[0]
    block_width = waves // block_count
    high = lax.Precision.HIGHEST

    lat_rows = lat_order.reshape(count, RQ, R5).transpose(2, 1, 0).reshape(2, lat_half).astype(F32)
    my_waves = lax.dynamic_slice_in_dim(wave_order, lax.axis_index("wave") * m_local, m_local)
    owner_rows = (
        my_waves[:, None] // block_width == jnp.arange(block_count, dtype=jnp.int32)[None, :]
    ).astype(F32)
    live_rows = jnp.dot(owner_rows, pattern.astype(F32), precision=high)
    live = jnp.repeat(live_rows, block_width, axis=1)
    rows_in = jnp.concatenate([live, lat_rows, lat_weight[None, :]], axis=0)
    places = jnp.concatenate([my_waves, lax.axis_index("lev")[None]]).astype(jnp.int32)

    einv_link = jnp.dot(einv, hydrostatic_thermal_link, precision=high)
    heat_evec = jnp.dot(spread_to_heat_link, evec, precision=high)
    gap = ((0, 0), (0, UNIT - FL), (0, 0))
    none = jnp.zeros((X, LEV, LOCAL), F32)
    tail = jnp.zeros((X, LEV, UNIT - FL), F32)
    first = jnp.concatenate(
        [
            jnp.concatenate([einv.reshape(X, LEV, LOCAL), none, tail], axis=2),
            jnp.concatenate([none, einv_link.reshape(X, LEV, LOCAL), tail], axis=2),
        ],
        axis=0,
    ).reshape(2 * X, XP)
    second = jnp.concatenate(
        [evec.reshape(LEV, LOCAL, X), -heat_evec.reshape(LEV, LOCAL, X)], axis=1
    )
    second = jnp.pad(second, gap).reshape(XP, X)
    place = jnp.arange(XP, dtype=jnp.int32) % UNIT
    keep = ((place >= LOCAL) & (place < FL)).astype(F32)[:, None]
    vert = stack_terms(first, second, keep, modes)

    def twin(matrix):
        rows, columns = matrix.shape
        down = jnp.arange(2 * rows, dtype=jnp.int32)[:, None]
        across = jnp.arange(2 * columns, dtype=jnp.int32)[None, :]
        left = (down // 2 == jnp.arange(rows, dtype=jnp.int32)[None, :]).astype(F32)
        right = (across // 2 == jnp.arange(columns, dtype=jnp.int32)[:, None]).astype(F32)
        spread = jnp.dot(jnp.dot(left, matrix, precision=high), right, precision=high)
        return jnp.where(down % 2 == across % 2, spread, 0.0)

    none = jnp.zeros((X, LEV, LOCAL), F32)
    fold = jnp.stack(
        [
            jnp.concatenate([einv.reshape(X, LEV, LOCAL), none], axis=2),
            jnp.concatenate([none, einv_link.reshape(X, LEV, LOCAL)], axis=2),
        ]
    ).reshape(2 * X, 2 * X)
    wide_first = twin(fold)
    spread = jnp.concatenate(
        [evec.reshape(LEV, LOCAL, X), -heat_evec.reshape(LEV, LOCAL, X)], axis=1
    ).reshape(2 * X, X)
    wide_second = twin(spread)
    place = (jnp.arange(XW, dtype=jnp.int32) % PAIR) // 2
    keep = (place >= LOCAL).astype(F32)[:, None]
    wide_vert = stack_terms(wide_first, wide_second, keep, jnp.repeat(modes, 2))

    vmem = pl.BlockSpec(memory_space=pltpu.VMEM)
    smem = pl.BlockSpec(memory_space=pltpu.SMEM)
    hbm = pl.BlockSpec(memory_space=pltpu.HBM)
    peers = count * LEV
    rowed = (FL, RQ * R5, 2, waves)
    block = jax.ShapeDtypeStruct((peers, ROWS, LANES), BF16)
    block_scratch = pltpu.VMEM((LANES // 128, peers * ROWS, 128), F32)

    sent = pl.pallas_call(
        select_kernel,
        in_specs=[vmem, hbm],
        out_specs=hbm,
        out_shape=block,
        scratch_shapes=[
            pltpu.VMEM(rowed, BF16),
            pltpu.VMEM((RQ, SIDE, waves), BF16),
            block_scratch,
            pltpu.VMEM(block.shape, BF16),
            pltpu.SemaphoreType.DMA((RQ,)),
            pltpu.SemaphoreType.DMA((CUTS,)),
        ],
        compiler_params=params(60),
        name="select_waves",
    )(wave_order, fourier.transpose(0, 2, 3, 1, 4).reshape(rowed))
    arrived = lax.all_to_all(sent, ("lev", "wave"), split_axis=0, concat_axis=0, tiled=True)
    solved = pl.pallas_call(
        spectral_kernel,
        in_specs=[smem] + [vmem] * 4 + [hbm],
        out_specs=vmem,
        out_shape=block,
        scratch_shapes=[
            pltpu.VMEM((lat_count, lat_count), BF16),
            block_scratch,
            pltpu.VMEM((TOTAL, lat_count), BF16),
            pltpu.VMEM((TOTAL, lat_half), BF16),
            pltpu.VMEM((TOTAL, lat_half), BF16),
            pltpu.VMEM((LEV, WIDE, RQ * count), F32),
            pltpu.VMEM((3,) + legendre.shape[1:], BF16),
            pltpu.SemaphoreType.DMA((3,)),
        ],
        compiler_params=params(46),
        name="spectral_round",
    )(places, arrived, rows_in, vert, wide_vert, legendre)
    returned = lax.all_to_all(solved, ("lev", "wave"), split_axis=0, concat_axis=0, tiled=True)
    restored = pl.pallas_call(
        restore_kernel,
        in_specs=[vmem] * 2,
        out_specs=hbm,
        out_shape=jax.ShapeDtypeStruct(rowed, BF16),
        scratch_shapes=[
            block_scratch,
            pltpu.VMEM(rowed, BF16),
            pltpu.SemaphoreType.DMA((RQ,)),
        ],
        compiler_params=params(48),
        name="restore_waves",
    )(wave_order, returned)
    restored = restored.reshape(2, LOCAL, RQ * R5, 2, waves)
    return restored.transpose(0, 3, 1, 2, 4)


def solution(mesh):
    placed = (
        P(None, None, "lev", "wave", None),
        P(),
        P(),
        P(),
        P("wave", None, None),
        P(),
        P(),
        P(),
        P(),
        P(),
        P(),
    )
    return jax.shard_map(
        local,
        mesh=mesh,
        in_specs=placed,
        out_specs=P(None, None, "lev", "wave", None),
        check_vma=False,
    )
```
